512 devices in a mesh: chan: 16 (over x, z_lo), win: 32 (over y, z_hi, core).
Axes of the slice: x: 4, y: 8, z: 8 (z_hi: 2, z_lo: 4; z = z_hi * 4 + z_lo), core: 2. Of those that a mesh axis runs over, the one named last changes fastest.
Arguments:
- spectra: bfloat16 [128, 512, 2, 1024], P('chan', 'win'), may hold values from -27 to 27, as said below
- pair_bin: int32 [128, 3, 8], P('chan'), may hold values from 0 to 127, as said below
- bin_owner: int32 [128], replicated, may hold values from 0 to 31, as said below
Outputs:
- owned: float32 [16, 224, 2, 1024], P('chan', 'win')
The draws below stay inside these ranges and needn't reach their ends.
Inputs may be any that keep to these rules, and one draw needn't show every extreme that they name: `spectra`: spectra are finite. `pair_bin`: every offset bin of 0 to 127 may occur. `bin_owner`: each index of win owns between 1 and 7 of the 128 bins, and at least one owns exactly 7.
All inputs are finite; a program needn't handle non-finite values.
Results may differ from the reference program's by a relative error of at most 0.0013.
Values may be sent and summed in bfloat16 or wider, within the bound.
A program may use at most 128 MiB of HBM per device.

```python
import math
import jax
import jax.numpy as jnp
from jax import lax

CH_DEV = 8
W_DEV = 16
F = 1024
REACH = 2
BINS_OWN = 4
CAP = 7
CHANNELS = 128
WINDOWS = 512
BINS = 128
SLOTS = 224
N_CHAN = 16


def draw_spectra(key, part):
    subkeys = jax.random.split(key, 3)
    extent = (CHANNELS, WINDOWS, 2, F)
    lower = math.log(0.3)
    upper = math.log(3.0)
    row_scale = jnp.exp(jax.random.uniform(subkeys[1], (CHANNELS, WINDOWS, 1, 1), jnp.float32, lower, upper))
    column_scale = jnp.exp(jax.random.uniform(subkeys[2], (1, 1, 1, F), jnp.float32, lower, upper))
    noise = jax.random.truncated_normal(subkeys[0], -3.0, 3.0, extent, jnp.float32)
    return (noise * row_scale * column_scale).astype(jnp.bfloat16)


def draw_pair_bin(key, part):
    subkeys = jax.random.split(key, 2)
    extent = (CHANNELS, REACH + 1, CH_DEV)
    channel = (jnp.arange(CHANNELS, dtype=jnp.int32) % CH_DEV)[:, None, None]
    reach_step = jnp.arange(REACH + 1, dtype=jnp.int32)[None, :, None]
    partner = jnp.arange(CH_DEV, dtype=jnp.int32)[None, None, :]
    jitter = jax.random.randint(subkeys[0], extent, -2, 3, dtype=jnp.int32)
    offset = reach_step * CH_DEV + partner - channel + jitter
    span_total = (REACH + 1) * CH_DEV
    dither = jax.random.randint(subkeys[1], extent, 0, BINS, dtype=jnp.int32)
    binned = (jnp.abs(offset) * BINS + dither) // span_total
    return jnp.minimum(binned, BINS - 1).astype(jnp.int32)


def draw_bin_owner(key, part):
    subkeys = jax.random.split(key, 3)
    owner_count = BINS // BINS_OWN
    halves = owner_count // 2
    excess = jax.random.randint(subkeys[0], (halves,), 1 - BINS_OWN, BINS_OWN, dtype=jnp.int32)
    excess = excess.at[0].set(BINS_OWN - 1)
    loads = jnp.concatenate([BINS_OWN + excess, BINS_OWN - excess])
    owners = jax.random.permutation(subkeys[1], owner_count).astype(jnp.int32)
    per_owner = jnp.zeros((owner_count,), jnp.int32).at[owners].set(loads)
    bounds = jnp.cumsum(per_owner)
    position = jnp.arange(BINS, dtype=jnp.int32)
    ordered = jnp.sum((bounds[None, :] <= position[:, None]).astype(jnp.int32), axis=1)
    shuffle = jax.random.permutation(subkeys[2], BINS).astype(jnp.int32)
    return ordered[shuffle].astype(jnp.int32)


def setup_inputs(seed: int = 0) -> dict:
    key_list = jax.random.split(jax.random.key(seed), 4)
    spectra = draw_spectra(jax.random.fold_in(key_list[3], 71), 0)
    pair_bin = draw_pair_bin(jax.random.fold_in(key_list[3], 71), 0)
    bin_owner = draw_bin_owner(jax.random.fold_in(key_list[3], 71), 0)
    return {"spectra": spectra, "pair_bin": pair_bin, "bin_owner": bin_owner}


def whiten(block_spectra):
    values = block_spectra.astype(jnp.float32)
    power = lax.optimization_barrier(jnp.mean(values * values, axis=(-2, -1), keepdims=True))
    return (values * lax.rsqrt(power + 1e-06)).astype(jnp.bfloat16)

def pair_stack(near_block, far_block, pair_map):
    rotated = jnp.stack([-far_block[:, :, 1], far_block[:, :, 0]], axis=2)
    partner = jnp.stack([far_block, rotated], axis=3)
    products = jnp.einsum('awcf,bwcjf->abjf', near_block.astype(jnp.float32), partner.astype(jnp.float32))
    rows_flat = products.reshape(CH_DEV * CH_DEV, 2, F)
    return jax.ops.segment_sum(rows_flat, pair_map.reshape(-1), num_segments=BINS)

def reference(spectra, pair_bin, bin_owner):
    shaped = spectra.reshape(N_CHAN, CH_DEV, WINDOWS, 2, F)
    white = lax.map(whiten, shaped)
    maps = pair_bin.reshape(N_CHAN, CH_DEV, REACH + 1, CH_DEV)

    def one_block(block_id):
        near_block = white[block_id]
        summed = jnp.zeros((BINS, 2, F), jnp.float32)
        for reach_step in range(REACH + 1):
            far_block = white[(block_id + reach_step) % N_CHAN]
            summed = summed + pair_stack(near_block, far_block, maps[block_id][:, reach_step, :])
        return summed
    stacks = lax.map(one_block, jnp.arange(N_CHAN, dtype=jnp.int32))
    factor = math.sqrt(BINS_OWN / (W_DEV * (REACH + 1) * CH_DEV * CH_DEV))
    scaled = stacks * factor
    ranking = jnp.arange(BINS, dtype=jnp.int32)
    shared_owner = bin_owner[None, :] == bin_owner[:, None]
    earlier = ranking[None, :] < ranking[:, None]
    position = lax.optimization_barrier(jnp.sum((shared_owner & earlier).astype(jnp.int32), axis=1))
    targets = bin_owner * CAP + position
    owned = jnp.zeros((N_CHAN, SLOTS, 2, F), jnp.float32).at[:, targets].set(scaled)
    return owned
```

```python
import functools
import math

import jax
import jax.numpy as jnp
from jax import lax
from jax.experimental import pallas as pl
from jax.experimental.pallas import tpu as pltpu
from jax.sharding import PartitionSpec as P

REACH = 2
BINS_OWN = 4
CAP = 7
EPS = 1e-06
F32 = jnp.float32
BF16 = jnp.bfloat16


def kernel(
    n_chan, factor,
    spec_ref, pair_ref, owner_ref, out_ref,
    white, afull, near1, near2, tmp, prods, selt, sel, pick, stack, cbuf,
    ysend, yrecv, yacc, zrecv, ufull, vslots, rbuf,
    s1, r1, s2, r2, cs, cr, ys, yr, zs, zr, us, ur, fs, fr,
):
    chan = lax.axis_index("chan")
    win = lax.axis_index("win")
    chip = win // 2
    core = win % 2
    y = chip // 2
    zh = chip % 2
    left = (chan + n_chan - 1) % n_chan
    right = (chan + 1) % n_chan
    sibling = win + 1 - 2 * core
    mesh_id = pl.DeviceIdType.MESH
    mine = pl.multiple_of(core * 64, 64)
    theirs = pl.multiple_of((1 - core) * 64, 64)

    barrier = pltpu.get_barrier_semaphore()
    for near in (left, right):
        pl.semaphore_signal(barrier, inc=1, device_id=(near, win), device_id_type=mesh_id)
    pl.semaphore_signal(barrier, inc=1, device_id=(chan, sibling), device_id_type=mesh_id)
    for o in range(1, 16):
        pl.semaphore_signal(
            barrier, inc=1, device_id=(chan, ((chip + o) % 16) * 2 + core), device_id_type=mesh_id
        )
    pl.semaphore_wait(barrier, 18)

    def remote(src, dst, send, recv, to):
        return pltpu.make_async_remote_copy(
            src_ref=src, dst_ref=dst, send_sem=send, recv_sem=recv, device_id=to, device_id_type=mesh_id
        )

    def hop1(k):
        return remote(white.at[k], near1.at[k], s1.at[k], r1.at[k], (left, win))

    def hop2(k):
        return remote(near1.at[k], near2.at[k], s2.at[k], r2.at[k], (left, win))

    def whiten(c, carry):
        x = spec_ref[c].astype(F32)
        power = jnp.sum(jnp.sum(x * x, axis=1, keepdims=True), axis=2, keepdims=True) * (1.0 / 2048.0)
        v = x * lax.rsqrt(power + EPS)
        tmp[...] = v.reshape(256, 128)
        re = tmp[pl.ds(0, 128, stride=2), :].reshape(16, 8, 128)
        im = tmp[pl.ds(1, 128, stride=2), :].reshape(16, 8, 128)
        wb = jnp.concatenate([re, im], axis=1).astype(BF16)
        white[c] = wb
        afull[c] = wb.astype(F32)
        hop1(c).start()
        return carry

    lax.fori_loop(0, 8, whiten, 0)

    def products(far, k):
        re = [None] * 8
        im = [None] * 8
        for w in range(16):
            b = far[k, w].astype(F32)
            br, bi = b[:8], b[8:]
            for c in range(8):
                ar = afull[c, w, 0:8, :]
                ai = afull[c, w, 8:16, :]
                pr = ar * br + ai * bi
                pi = ai * br - ar * bi
                re[c] = pr if w == 0 else re[c] + pr
                im[c] = pi if w == 0 else im[c] + pi
        for c in range(8):
            row = pl.multiple_of((k * 8 + c) * 16, 16)
            prods[pl.ds(row, 8), :] = re[c]
            prods[pl.ds(row + 8, 8), :] = im[c]

    def gather_bins(d, h):
        rows = jnp.concatenate(
            [prods[pl.ds(2 * h, 64, stride=16), :], prods[pl.ds(2 * h + 1, 64, stride=16), :]], axis=1
        )
        hi = rows.astype(BF16)
        lo = (rows - hi.astype(F32)).astype(BF16)
        both = jnp.concatenate([hi, lo], axis=0)
        t = jnp.dot(sel[d], both, preferred_element_type=F32)
        if d == 0:
            stack[2 * h] = t[:, :128]
            stack[2 * h + 1] = t[:, 128:]
        else:
            stack[2 * h] += t[:, :128]
            stack[2 * h + 1] += t[:, 128:]

    lanes = lax.broadcasted_iota(jnp.int32, (1, 128), 1)
    for d in range(REACH + 1):
        def fill(j, carry, d=d):
            hit = jnp.where(lanes == pair_ref[j % 8, d, j // 8], 1.0, 0.0)
            selt[pl.ds(j, 1), :] = hit
            selt[pl.ds(j + 64, 1), :] = hit
            return carry

        lax.fori_loop(0, 64, fill, 0)
        sel[d] = selt[...].T.astype(BF16)

    def own(k, carry):
        products(white, k)
        return carry

    lax.fori_loop(0, 8, own, 0)
    for h in range(8):
        gather_bins(0, h)

    def step1(k, carry):
        hop1(k).wait_recv()
        hop2(k).start()
        products(near1, k)
        return carry

    lax.fori_loop(0, 8, step1, 0)
    for h in range(8):
        gather_bins(1, h)

    owner = owner_ref[...]
    across = jnp.broadcast_to(owner.astype(F32), (128, 128))
    down = across.T
    rows_i = lax.broadcasted_iota(jnp.int32, (128, 128), 0)
    cols_i = lax.broadcasted_iota(jnp.int32, (128, 128), 1)
    ahead = jnp.where((across == down) & (rows_i < cols_i), 1.0, 0.0)
    rank = jnp.sum(ahead, axis=0, keepdims=True)
    slot = owner.astype(F32) * 8.0 + rank
    wanted = ((rows_i >> 3) * 2 + core) * 8 + (rows_i & 7)
    pick[...] = jnp.where(wanted.astype(F32) == slot, 1.0, 0.0)

    def step2(k, carry):
        hop2(k).wait_recv()
        products(near2, k)
        return carry

    lax.fori_loop(0, 8, step2, 0)

    def core_copy(h):
        return remote(
            stack.at[pl.ds(2 * h, 2), pl.ds(theirs, 64), :], cbuf.at[pl.ds(2 * h, 2)],
            cs.at[h], cr.at[h], (chan, sibling),
        )

    for h in range(8):
        gather_bins(2, h)
        core_copy(h).start()

    def y_copy(o):
        to = (y + o) % 8
        return remote(
            ysend.at[o - 1], yrecv.at[o - 1], ys.at[o - 1], yr.at[o - 1],
            (chan, to * 4 + zh * 2 + core),
        )

    scale = 1.0 + chip.astype(F32) * 0.0625
    acc = None
    for o in (4, 3, 5, 2, 6, 1, 7, 0):
        h = (y + o) % 8
        core_copy(h).wait_recv()
        t = stack[pl.ds(2 * h, 2), pl.ds(mine, 64), :] + cbuf[pl.ds(2 * h, 2)]
        if o:
            ysend[o - 1] = (t * scale).astype(BF16)
            y_copy(o).start()
        else:
            acc = t
    for o in (1, 7, 2, 6, 3, 5, 4):
        source = ((y + 8 - o) % 8) * 2 + zh
        y_copy(o).wait_recv()
        acc = acc + yrecv[o - 1].astype(F32) * (1.0 / (1.0 + source.astype(F32) * 0.0625))
    yacc[...] = acc
    z_copy = remote(yacc.at[1 - zh], zrecv, zs, zr, (chan, y * 4 + (1 - zh) * 2 + core))
    z_copy.start()
    z_copy.wait_recv()
    ufull[pl.ds(mine, 64), :] = yacc[zh] + zrecv[...]
    u_copy = remote(ufull.at[pl.ds(mine, 64)], ufull.at[pl.ds(mine, 64)], us, ur, (chan, sibling))
    u_copy.start()
    u_copy.wait_recv()
    v = jnp.dot(pick[...], ufull[...], precision=lax.Precision.HIGHEST, preferred_element_type=F32)
    vslots[...] = (v * factor).reshape(16, 8, 128)

    def slot_copy(o, src, dst, to):
        return remote(vslots.at[src], rbuf.at[dst], fs.at[o - 1], fr.at[o - 1], (chan, to * 2 + core))

    for o in range(1, 16):
        to = (chip + o) % 16
        slot_copy(o, to, chip, to).start()
    rbuf[chip] = vslots[chip]
    for o in range(1, 16):
        slot_copy(o, (chip + o) % 16, (chip + 16 - o) % 16, (chip + o) % 16).wait_recv()
    out_ref[...] = rbuf[...]

    for k in range(8):
        hop1(k).wait_send()
        hop2(k).wait_send()
        core_copy(k).wait_send()
    for o in range(1, 8):
        y_copy(o).wait_send()
    z_copy.wait_send()
    u_copy.wait_send()
    for o in range(1, 16):
        to = (chip + o) % 16
        slot_copy(o, to, chip, to).wait_send()


def shards(n_chan, spectra, pair_bin, bin_owner):
    channels, windows, _, freqs = spectra.shape
    factor = math.sqrt(BINS_OWN / (windows * (REACH + 1) * channels * channels))
    rows = spectra.reshape(channels, windows, 2, freqs // 128, 128)
    rows = rows.transpose(0, 1, 3, 2, 4).reshape(channels, windows, 16, 128)
    vmem = pl.BlockSpec(memory_space=pltpu.VMEM)
    dma = pltpu.SemaphoreType.DMA
    block = (8, 16, 16, 128)
    out = pl.pallas_call(
        functools.partial(kernel, n_chan, factor),
        out_shape=jax.ShapeDtypeStruct((16, 8, 128), F32),
        in_specs=[vmem, pl.BlockSpec(memory_space=pltpu.SMEM), vmem],
        out_specs=vmem,
        scratch_shapes=[
            pltpu.VMEM(block, BF16),
            pltpu.VMEM(block, F32),
            pltpu.VMEM(block, BF16),
            pltpu.VMEM(block, BF16),
            pltpu.VMEM((256, 128), F32),
            pltpu.VMEM((1024, 128), F32),
            pltpu.VMEM((128, 128), F32),
            pltpu.VMEM((3, 128, 128), BF16),
            pltpu.VMEM((128, 128), F32),
            pltpu.VMEM((16, 128, 128), F32),
            pltpu.VMEM((16, 64, 128), F32),
            pltpu.VMEM((7, 2, 64, 128), BF16),
            pltpu.VMEM((7, 2, 64, 128), BF16),
            pltpu.VMEM((2, 64, 128), F32),
            pltpu.VMEM((64, 128), F32),
            pltpu.VMEM((128, 128), F32),
            pltpu.VMEM((16, 8, 128), F32),
            pltpu.VMEM((16, 8, 128), F32),
            dma((8,)), dma((8,)), dma((8,)), dma((8,)), dma((8,)), dma((8,)),
            dma((7,)), dma((7,)), dma, dma, dma, dma, dma((15,)), dma((15,)),
        ],
        compiler_params=pltpu.CompilerParams(
            collective_id=0, has_side_effects=True, vmem_limit_bytes=32 * 1024 * 1024
        ),
    )(rows, pair_bin, bin_owner.reshape(1, 128))
    out = out[:, :CAP].reshape(2, 8, CAP, 128).transpose(2, 0, 1, 3)
    return out.reshape(1, CAP, 2, freqs)


def solution(mesh):
    in_specs = (P("chan", "win", None, None), P("chan", None, None), P())
    out_specs = P("chan", "win", None, None)
    body = functools.partial(shards, mesh.shape["chan"])
    return jax.shard_map(body, mesh=mesh, in_specs=in_specs, out_specs=out_specs, check_vma=False)
```

```python
import functools
import math

import jax
import jax.numpy as jnp
from jax import lax
from jax.experimental import pallas as pl
from jax.experimental.pallas import tpu as pltpu
from jax.sharding import PartitionSpec as P

REACH = 2
BINS_OWN = 4
CAP = 7
EPS = 1e-06
CHUNK = 2
F32 = jnp.float32
BF16 = jnp.bfloat16
FAR_FIRST = (4, 3, 5, 2, 6, 1, 7)


def kernel(
    n_chan, factor,
    spec_hbm, pair_ref, owner_ref, out_ref,
    spec, tmp, wsend, full, afull, near1, near2, prods, selt, sel, pick, stack, cbuf, vslots, rbuf,
    ins, ats, atr, s1, r1, s2, r2, cs, cr, fs, fr,
):
    chan = lax.axis_index("chan")
    win = lax.axis_index("win")
    core = win % 2
    y = win // 4
    inner = win % 4
    left = (chan + n_chan - 1) % n_chan
    right = (chan + 1) % n_chan
    sibling = win + 1 - 2 * core
    mesh_id = pl.DeviceIdType.MESH

    barrier = pltpu.get_barrier_semaphore()
    for near in (left, right):
        pl.semaphore_signal(barrier, inc=1, device_id=(near, win), device_id_type=mesh_id)
    for o in range(1, 32):
        pl.semaphore_signal(barrier, inc=1, device_id=(chan, (win + o) % 32), device_id_type=mesh_id)

    def load(c):
        return pltpu.make_async_copy(spec_hbm.at[c], spec.at[c], ins.at[c])

    for c in range(8):
        load(c).start()

    def remote(src, dst, send, recv, to):
        return pltpu.make_async_remote_copy(
            src_ref=src, dst_ref=dst, send_sem=send, recv_sem=recv, device_id=to, device_id_type=mesh_id
        )

    def spread(j, o, origin):
        to = (y + o) % 8
        rows = pl.multiple_of(origin * 16, 16)
        n = j * 7 + o - 1
        return remote(
            wsend.at[to, pl.ds(CHUNK * j, CHUNK)],
            full.at[pl.ds(CHUNK * j, CHUNK), :, pl.ds(rows, 16), :],
            ats.at[n], atr.at[n], (chan, to * 4 + inner),
        )

    def hop1(k):
        return remote(full.at[k], near1.at[k], s1.at[k], r1.at[k], (left, win))

    def hop2(k):
        return remote(near1.at[k], near2.at[k], s2.at[k], r2.at[k], (left, win))

    def whiten(c):
        load(c).wait()
        x = spec[c].astype(F32)
        power = jnp.sum(jnp.sum(x * x, axis=1, keepdims=True), axis=2, keepdims=True) * (1.0 / 2048.0)
        tmp[c % 2] = (x * lax.rsqrt(power + EPS)).reshape(256, 128)
        for t in range(8):
            for p in range(2):
                wsend[t, c, p] = tmp[c % 2, pl.ds(2 * t + p, 16, stride=16), :].astype(BF16)

    own_rows = pl.multiple_of(y * 16, 16)
    for j in range(8 // CHUNK):
        for c in range(CHUNK * j, CHUNK * j + CHUNK):
            whiten(c)
        if j == 0:
            pl.semaphore_wait(barrier, 33)
        for o in FAR_FIRST:
            spread(j, o, y).start()
        part = slice(CHUNK * j, CHUNK * j + CHUNK)
        full[part, :, pl.ds(own_rows, 16), :] = wsend[y, part]

    lanes = lax.broadcasted_iota(jnp.int32, (8, 128), 1)

    def select(d):
        def fill(j, carry):
            row = pl.multiple_of(j * 8, 8)
            selt[pl.ds(row, 8), :] = jnp.where(lanes == pair_ref[d, j % 8, j // 8], 1.0, 0.0)
            return carry

        lax.fori_loop(0, 64, fill, 0)
        sel[d] = selt[...].T.astype(BF16)

    for j in range(8 // CHUNK):
        if j < REACH + 1:
            select(j)
        for o in FAR_FIRST[::-1]:
            spread(j, o, (y + 8 - o) % 8).wait_recv()
        for k in range(CHUNK * j, CHUNK * j + CHUNK):
            hop1(k).start()
        if j:
            for k in range(CHUNK * j - CHUNK, CHUNK * j):
                hop1(k).wait_recv()
                hop2(k).start()
        part = slice(CHUNK * j, CHUNK * j + CHUNK)
        afull[part] = full[part].astype(F32)

    def products(far, k):
        re = [None] * 8
        im = [None] * 8
        for g in range(8):
            wide_r = far[k, 0, 16 * g:16 * g + 16, :].astype(F32)
            wide_i = far[k, 1, 16 * g:16 * g + 16, :].astype(F32)
            for h in range(2):
                br, bi = wide_r[8 * h:8 * h + 8], wide_i[8 * h:8 * h + 8]
                w = 16 * g + 8 * h
                for c in range(8):
                    ar = afull[c, 0, w:w + 8, :]
                    ai = afull[c, 1, w:w + 8, :]
                    pr = ar * br + ai * bi
                    pi = ai * br - ar * bi
                    re[c] = pr if w == 0 else re[c] + pr
                    im[c] = pi if w == 0 else im[c] + pi
        for c in range(8):
            row = pl.multiple_of((k * 8 + c) * 8, 8)
            prods[0, pl.ds(row, 8), :] = re[c]
            prods[1, pl.ds(row, 8), :] = im[c]

    def gather_bins(d):
        rows = jnp.concatenate([prods[0], prods[1]], axis=1)
        hi = rows.astype(BF16)
        lo = (rows - hi.astype(F32)).astype(BF16)
        t = jnp.dot(sel[d], hi, preferred_element_type=F32) + jnp.dot(sel[d], lo, preferred_element_type=F32)
        if d == 0:
            stack[0] = t[:, :128]
            stack[1] = t[:, 128:]
        else:
            stack[0] += t[:, :128]
            stack[1] += t[:, 128:]

    for k in range(8 - CHUNK, 8):
        hop1(k).wait_recv()
        hop2(k).start()

    def own(k, carry):
        products(full, k)
        return carry

    lax.fori_loop(0, 8, own, 0)
    gather_bins(0)

    def step1(k, carry):
        products(near1, k)
        return carry

    lax.fori_loop(0, 8, step1, 0)
    gather_bins(1)

    owner = owner_ref[...].astype(F32)
    across = jnp.broadcast_to(owner, (128, 128))
    down = across.T
    rows_i = lax.broadcasted_iota(jnp.int32, (128, 128), 0)
    cols_i = lax.broadcasted_iota(jnp.int32, (128, 128), 1)
    ahead = jnp.where((across == down) & (rows_i < cols_i), 1.0, 0.0)
    slot = owner * 8.0 + jnp.sum(ahead, axis=0, keepdims=True)
    wanted = lax.broadcasted_iota(jnp.int32, (256, 128), 0).astype(F32)
    hit = jnp.where(wanted == slot, 1.0, 0.0).astype(BF16)
    pick[...] = jnp.concatenate([hit, hit], axis=1)

    def step2(k, carry):
        hop2(k).wait_recv()
        products(near2, k)
        return carry

    lax.fori_loop(0, 8, step2, 0)
    gather_bins(2)

    core_copy = remote(stack.at[1 - core], cbuf, cs, cr, (chan, sibling))
    core_copy.start()
    core_copy.wait_recv()
    total = (stack[core] + cbuf[...]) * factor
    hi = total.astype(BF16)
    lo = (total - hi.astype(F32)).astype(BF16)
    v = jnp.dot(pick[...], jnp.concatenate([hi, lo], axis=0), preferred_element_type=F32)
    vslots[...] = v.reshape(32, 8, 128)

    def slot_copy(o, origin):
        to = (win + o) % 32
        return remote(vslots.at[to], rbuf.at[origin], fs.at[o - 1], fr.at[o - 1], (chan, to))

    def send_slots(i, carry):
        o = (i + 16) % 31 + 1
        slot_copy(o, win).start()
        return carry

    lax.fori_loop(0, 31, send_slots, 0)
    rbuf[win] = vslots[win]

    def take_slots(i, carry):
        o = i + 1
        slot_copy(o, (win + 32 - o) % 32).wait_recv()
        return carry

    lax.fori_loop(0, 31, take_slots, 0)
    for t in range(8):
        for p in range(2):
            out_ref[p * 8 + t] = rbuf[t * 4 + p] + rbuf[t * 4 + 2 + p]

    for j in range(8 // CHUNK):
        for o in FAR_FIRST:
            spread(j, o, y).wait_send()
    for k in range(8):
        hop1(k).wait_send()
        hop2(k).wait_send()
    core_copy.wait_send()

    def finish(i, carry):
        slot_copy(i + 1, win).wait_send()
        return carry

    lax.fori_loop(0, 31, finish, 0)


def shards(n_chan, spectra, pair_bin, bin_owner):
    channels, windows, _, freqs = spectra.shape
    factor = math.sqrt(BINS_OWN / (windows * (REACH + 1) * channels * channels))
    rows = spectra.reshape(channels, windows, 2, freqs // 128, 128)
    rows = rows.transpose(0, 1, 3, 2, 4).reshape(channels, windows, 16, 128)
    vmem = pl.BlockSpec(memory_space=pltpu.VMEM)
    dma = pltpu.SemaphoreType.DMA
    block = (8, 2, 128, 128)
    out = pl.pallas_call(
        functools.partial(kernel, n_chan, factor),
        out_shape=jax.ShapeDtypeStruct((16, 8, 128), F32),
        in_specs=[pl.BlockSpec(memory_space=pl.ANY), pl.BlockSpec(memory_space=pltpu.SMEM), vmem],
        out_specs=vmem,
        scratch_shapes=[
            pltpu.VMEM((8, 16, 16, 128), BF16),
            pltpu.VMEM((2, 256, 128), F32),
            pltpu.VMEM((8, 8, 2, 16, 128), BF16),
            pltpu.VMEM(block, BF16),
            pltpu.VMEM(block, F32),
            pltpu.VMEM(block, BF16),
            pltpu.VMEM(block, BF16),
            pltpu.VMEM((2, 512, 128), F32),
            pltpu.VMEM((512, 128), F32),
            pltpu.VMEM((3, 128, 512), BF16),
            pltpu.VMEM((256, 256), BF16),
            pltpu.VMEM((2, 128, 128), F32),
            pltpu.VMEM((128, 128), F32),
            pltpu.VMEM((32, 8, 128), F32),
            pltpu.VMEM((32, 8, 128), F32),
            dma((8,)), dma((28,)), dma((28,)), dma((8,)), dma((8,)), dma((8,)), dma((8,)),
            dma, dma, dma((31,)), dma((31,)),
        ],
        compiler_params=pltpu.CompilerParams(
            collective_id=0, has_side_effects=True, vmem_limit_bytes=32 * 1024 * 1024
        ),
    )(rows, pair_bin.transpose(1, 0, 2), bin_owner.reshape(1, 128))
    out = out[:, :CAP].reshape(2, 8, CAP, 128).transpose(2, 0, 1, 3)
    return out.reshape(1, CAP, 2, freqs)


def solution(mesh):
    in_specs = (P("chan", "win", None, None), P("chan", None, None), P())
    out_specs = P("chan", "win", None, None)
    body = functools.partial(shards, mesh.shape["chan"])
    return jax.shard_map(body, mesh=mesh, in_specs=in_specs, out_specs=out_specs, check_vma=False)
```

```python
import functools
import math

import jax
import jax.numpy as jnp
from jax import lax
from jax.experimental import pallas as pl
from jax.experimental.pallas import tpu as pltpu
from jax.sharding import PartitionSpec as P

REACH = 2
BINS_OWN = 4
CAP = 7
EPS = 1e-06
F32 = jnp.float32
BF16 = jnp.bfloat16
CHUNK = 2
PARTS = 8 // CHUNK
PACE = 4
LAG = 2
FAR_FIRST = (4, 3, 5, 2, 6, 1, 7)


def kernel(
    n_chan, factor,
    spec_hbm, pair_ref, owner_ref, out_ref,
    spec, tmp, wsend, full, afull, near1, near2, prods, selt, pick, comb, vbuf, cbuf, rbuf,
    ins, ats, atr, s1, r1, s2, r2, cs, cr, fs, fr,
):
    chan = lax.axis_index("chan")
    win = lax.axis_index("win")
    core = win % 2
    chip = win // 2
    y = chip // 2
    zh = chip % 2
    left = (chan + n_chan - 1) % n_chan
    right = (chan + 1) % n_chan
    sibling = win + 1 - 2 * core
    mesh_id = pl.DeviceIdType.MESH

    barrier = pltpu.get_barrier_semaphore()
    for near in (left, right):
        pl.semaphore_signal(barrier, inc=1, device_id=(near, win), device_id_type=mesh_id)
    pl.semaphore_signal(barrier, inc=1, device_id=(chan, sibling), device_id_type=mesh_id)
    for o in range(1, 16):
        pl.semaphore_signal(
            barrier, inc=1, device_id=(chan, ((chip + o) % 16) * 2 + core), device_id_type=mesh_id
        )

    def load(c):
        return pltpu.make_async_copy(spec_hbm.at[c], spec.at[c], ins.at[c])

    for c in range(8):
        load(c).start()

    def remote(src, dst, send, recv, to):
        return pltpu.make_async_remote_copy(
            src_ref=src, dst_ref=dst, send_sem=send, recv_sem=recv, device_id=to, device_id_type=mesh_id
        )

    def spread(j, o):
        to = (y + o) % 8
        part = slice(CHUNK * j, CHUNK * j + CHUNK)
        m = j * 7 + o - 1
        return remote(
            wsend.at[to, part], full.at[part, :, 16 * o:16 * o + 16, :],
            ats.at[m], atr.at[m], (chan, to * 4 + zh * 2 + core),
        )

    def cut(ref, j):
        if j == PARTS:
            return ref.at[:, :, 0:16, :]
        return ref.at[CHUNK * j:CHUNK * j + CHUNK, :, 16:128, :]

    def hop1(j):
        return remote(cut(full, j), cut(near1, j), s1.at[j], r1.at[j], (left, win))

    def hop2(j):
        return remote(cut(near1, j), cut(near2, j), s2.at[j], r2.at[j], (left, win))

    def whiten(c):
        load(c).wait()
        x = spec[c].astype(F32)
        power = jnp.sum(jnp.sum(x * x, axis=1, keepdims=True), axis=2, keepdims=True) * (1.0 / 2048.0)
        tmp[c % 2] = (x * lax.rsqrt(power + EPS)).reshape(256, 128)
        for t in range(8):
            for p in range(2):
                wsend[t, c, p] = tmp[c % 2, pl.ds(2 * t + p, 16, stride=16), :].astype(BF16)

    def send_part(j):
        for o in FAR_FIRST:
            spread(j, o).start()

    for j in range(PARTS):
        for c in range(CHUNK * j, CHUNK * j + CHUNK):
            whiten(c)
        if j == 0:
            pl.semaphore_wait(barrier, 18)
        if j < PACE:
            send_part(j)
    full[:, :, 0:16, :] = wsend[y]
    hop1(PARTS).start()

    lanes = lax.broadcasted_iota(jnp.int32, (8, 128), 1)

    def select(d):
        def fill(j, carry):
            row = pl.multiple_of(j * 8, 8)
            selt[d, pl.ds(row, 8), :] = jnp.where(lanes == pair_ref[d, j % 8, j // 8], 1.0, 0.0)
            return carry

        lax.fori_loop(0, 64, fill, 0)

    def find_slots():
        owner = owner_ref[...].astype(F32)
        across = jnp.broadcast_to(owner, (128, 128))
        down = across.T
        rows_i = lax.broadcasted_iota(jnp.int32, (128, 128), 0)
        cols_i = lax.broadcasted_iota(jnp.int32, (128, 128), 1)
        ahead = jnp.where((across == down) & (rows_i < cols_i), 1.0, 0.0)
        slot = owner * 8.0 + jnp.sum(ahead, axis=0, keepdims=True)
        r = lax.broadcasted_iota(jnp.int32, (256, 128), 0)
        wanted = (((r >> 3) & 7) * 4 + ((r >> 6) & 1) * 2 + (r >> 7)) * 8 + (r & 7)
        pick[...] = jnp.where(wanted.astype(F32) == slot, 1.0, 0.0).astype(BF16)

    def combine(d):
        comb[d] = jnp.dot(
            pick[...], selt[d].T.astype(BF16), preferred_element_type=F32
        ).astype(BF16)

    def products(d, far, part):
        def body(k, carry):
            re = [None] * 8
            im = [None] * 8
            for g in range(8):
                wide_r = far[k, 0, 16 * g:16 * g + 16, :].astype(F32)
                wide_i = far[k, 1, 16 * g:16 * g + 16, :].astype(F32)
                for h in range(2):
                    br, bi = wide_r[8 * h:8 * h + 8], wide_i[8 * h:8 * h + 8]
                    w = 16 * g + 8 * h
                    for c in range(8):
                        ar = afull[c, 0, w:w + 8, :]
                        ai = afull[c, 1, w:w + 8, :]
                        pr = ar * br + ai * bi
                        pi = ai * br - ar * bi
                        re[c] = pr if w == 0 else re[c] + pr
                        im[c] = pi if w == 0 else im[c] + pi
            for c in range(8):
                row = pl.multiple_of((k * 8 + c) * 8, 8)
                prods[d, 0, pl.ds(row, 8), :] = re[c]
                prods[d, 1, pl.ds(row, 8), :] = im[c]
            return carry

        lax.fori_loop(part.start, part.stop, body, 0)

    def slots_of(d):
        rows = jnp.concatenate([prods[d, 0], prods[d, 1]], axis=1)
        hi = rows.astype(BF16)
        lo = (rows - hi.astype(F32)).astype(BF16)
        return jnp.dot(comb[d], hi, preferred_element_type=F32) + jnp.dot(
            comb[d], lo, preferred_element_type=F32
        )

    def store_slots(v):
        for p in range(2):
            vbuf[:, :, :, p] = v[:, 128 * p:128 * p + 128].reshape(2, 2, 8, 8, 128)

    def forward(j):
        hop1(j).wait_recv()
        hop2(j).start()

    select(0)
    for j in range(PARTS):
        part = slice(CHUNK * j, CHUNK * j + CHUNK)
        for o in FAR_FIRST[::-1]:
            spread(j, o).wait_recv()
        hop1(j).start()
        if j + PACE < PARTS:
            send_part(j + PACE)
        if j == 0:
            forward(PARTS)
        if j >= LAG:
            forward(j - LAG)
        afull[part] = full[part].astype(F32)
    select(1)
    for j in range(PARTS - LAG, PARTS):
        forward(j)
    products(0, full, slice(0, 8))
    select(2)
    find_slots()
    for d in range(3):
        combine(d)
    v = slots_of(0)
    products(1, near1, slice(0, 8))
    v = v + slots_of(1)
    hop2(PARTS).wait_recv()
    for j in range(PARTS):
        hop2(j).wait_recv()
        products(2, near2, slice(CHUNK * j, CHUNK * j + CHUNK))
    store_slots((v + slots_of(2)) * factor)

    def core_copy(i):
        z = 1 - zh if i == 0 else zh
        return remote(vbuf.at[1 - core, z], cbuf.at[z], cs.at[i], cr.at[i], (chan, sibling))

    def slot_copy(i, dy, at, origin):
        z = 1 - zh if i == 0 else zh
        to = (y + dy) % 8
        m = 8 * i + dy
        return remote(
            vbuf.at[core, z, to], rbuf.at[at, origin], fs.at[m], fr.at[m],
            (chan, to * 4 + z * 2 + core),
        )

    for i in range(2):
        core_copy(i).start()
    for i in range(2):
        z = 1 - zh if i == 0 else zh
        core_copy(i).wait_recv()
        vbuf[core, z] += cbuf[z]
        for dy in (4, 3, 5, 2, 6, 1, 7, 0):
            if dy or i == 0:
                slot_copy(i, dy, zh, y).start()
    rbuf[zh, y] = vbuf[core, zh, y]
    for i in (1, 0):
        for dy in (1, 7, 2, 6, 3, 5, 4, 0):
            if dy or i == 0:
                slot_copy(i, dy, 1 - zh if i == 0 else zh, (y + 8 - dy) % 8).wait_recv()
    for t in range(8):
        for p in range(2):
            out_ref[p * 8 + t] = rbuf[0, t, p] + rbuf[1, t, p]

    for j in range(PARTS):
        for o in FAR_FIRST:
            spread(j, o).wait_send()
    for j in range(PARTS + 1):
        hop1(j).wait_send()
        hop2(j).wait_send()
    for i in range(2):
        core_copy(i).wait_send()
        for dy in range(8):
            if dy or i == 0:
                slot_copy(i, dy, zh, y).wait_send()


def shards(n_chan, spectra, pair_bin, bin_owner):
    channels, windows, _, freqs = spectra.shape
    factor = math.sqrt(BINS_OWN / (windows * (REACH + 1) * channels * channels))
    rows = spectra.reshape(channels, windows, 2, freqs // 128, 128)
    rows = rows.transpose(0, 1, 3, 2, 4).reshape(channels, windows, 16, 128)
    vmem = pl.BlockSpec(memory_space=pltpu.VMEM)
    dma = pltpu.SemaphoreType.DMA
    block = (8, 2, 128, 128)
    out = pl.pallas_call(
        functools.partial(kernel, n_chan, factor),
        out_shape=jax.ShapeDtypeStruct((16, 8, 128), F32),
        in_specs=[pl.BlockSpec(memory_space=pl.ANY), pl.BlockSpec(memory_space=pltpu.SMEM), vmem],
        out_specs=vmem,
        scratch_shapes=[
            pltpu.VMEM((8, 16, 16, 128), BF16),
            pltpu.VMEM((2, 256, 128), F32),
            pltpu.VMEM((8, 8, 2, 16, 128), BF16),
            pltpu.VMEM(block, BF16),
            pltpu.VMEM(block, F32),
            pltpu.VMEM(block, BF16),
            pltpu.VMEM(block, BF16),
            pltpu.VMEM((3, 2, 512, 128), F32),
            pltpu.VMEM((3, 512, 128), F32),
            pltpu.VMEM((256, 128), BF16),
            pltpu.VMEM((3, 256, 512), BF16),
            pltpu.VMEM((2, 2, 8, 2, 8, 128), F32),
            pltpu.VMEM((2, 8, 2, 8, 128), F32),
            pltpu.VMEM((2, 8, 2, 8, 128), F32),
            dma((8,)), dma((7 * PARTS,)), dma((7 * PARTS,)),
            dma((PARTS + 1,)), dma((PARTS + 1,)), dma((PARTS + 1,)), dma((PARTS + 1,)),
            dma((2,)), dma((2,)), dma((16,)), dma((16,)),
        ],
        compiler_params=pltpu.CompilerParams(
            collective_id=0, has_side_effects=True, vmem_limit_bytes=60 * 1024 * 1024
        ),
    )(rows, pair_bin.transpose(1, 0, 2), bin_owner.reshape(1, 128))
    out = out[:, :CAP].reshape(2, 8, CAP, 128).transpose(2, 0, 1, 3)
    return out.reshape(1, CAP, 2, freqs)


def solution(mesh):
    in_specs = (P("chan", "win", None, None), P("chan", None, None), P())
    out_specs = P("chan", "win", None, None)
    body = functools.partial(shards, mesh.shape["chan"])
    return jax.shard_map(body, mesh=mesh, in_specs=in_specs, out_specs=out_specs, check_vma=False)
```

```python
import functools
import math

import jax
import jax.numpy as jnp
from jax import lax
from jax.experimental import pallas as pl
from jax.experimental.pallas import tpu as pltpu
from jax.sharding import PartitionSpec as P

REACH = 2
BINS_OWN = 4
CAP = 7
EPS = 1e-06
F32 = jnp.float32
BF16 = jnp.bfloat16


def kernel(
    n_chan, factor,
    spec_hbm, pair_ref, owner_ref, out_ref,
    spec, tmp, wsend, line, ahead_line, near, sums, msg, rin, selt, pick, comb, vbuf, cbuf, rbuf,
    ins, ats, atr, xs, xr, ms, mr, cs, cr, fs, fr,
):
    chan = lax.axis_index("chan")
    win = lax.axis_index("win")
    x = chan // 4
    z = chan % 4
    core = win % 2
    chip = win // 2
    y = chip // 2
    zh = chip % 2
    inner = win % 4
    n_x = n_chan // 4
    x_left = (x + n_x - 1) % n_x
    x_right = (x + 1) % n_x
    sibling = win + 1 - 2 * core
    mesh_id = pl.DeviceIdType.MESH

    barrier = pltpu.get_barrier_semaphore()

    def greet(c, w):
        pl.semaphore_signal(barrier, inc=1, device_id=(c, w), device_id_type=mesh_id)

    for c in range(8):
        pltpu.make_async_copy(spec_hbm.at[c], spec.at[c], ins.at[c]).start()
    for near_x in (x_left, x_right):
        greet(near_x * 4 + z, win)
    greet(chan, sibling)
    for oy in range(8):
        for oz in range(4):
            if oy or oz:
                greet(x * 4 + (z + oz) % 4, ((y + oy) % 8) * 4 + inner)
        greet(chan, ((y + oy) % 8) * 4 + (1 - zh) * 2 + core)

    def remote(src, dst, send, recv, to):
        return pltpu.make_async_remote_copy(
            src_ref=src, dst_ref=dst, send_sem=send, recv_sem=recv, device_id=to, device_id_type=mesh_id
        )

    def spread(oy, oz, yo, zo):
        yt = (y + oy) % 8
        zt = (z + oz) % 4
        m = oy * 4 + oz
        return remote(
            wsend.at[yt, zt], line.at[zo, yo], ats.at[m], atr.at[m], (x * 4 + zt, yt * 4 + inner)
        )

    def onward(b, oy):
        yo = (y + 8 - oy) % 8
        m = b * 8 + oy
        return remote(line.at[b, yo], ahead_line.at[b, yo], xs.at[m], xr.at[m], (x_left * 4 + z, win))

    lane_block = lax.broadcasted_iota(jnp.int32, (8, 128), 1) >> 5
    top = lax.broadcasted_iota(jnp.int32, (8, 128), 0) < 4

    def whiten(cp):
        for i in range(2):
            c = 2 * cp + i
            pltpu.make_async_copy(spec_hbm.at[c], spec.at[c], ins.at[c]).wait()
            v = spec[c].astype(F32)
            power = jnp.sum(jnp.sum(v * v, axis=1, keepdims=True), axis=2, keepdims=True) * (1.0 / 2048.0)
            tmp[i] = (v * lax.rsqrt(power + EPS)).reshape(256, 128)
        for t in range(8):
            both = []
            for i in range(2):
                rl = tmp[i, pl.ds(2 * t, 8, stride=16), :]
                il = tmp[i, pl.ds(2 * t + 1, 8, stride=16), :]
                rh = tmp[i, pl.ds(128 + 2 * t, 8, stride=16), :]
                ih = tmp[i, pl.ds(129 + 2 * t, 8, stride=16), :]
                groups = [
                    jnp.where(top, rl, pltpu.roll(il, 4, 0)),
                    pltpu.roll(jnp.where(top, pltpu.roll(rl, 4, 0), il), 32, 1),
                    pltpu.roll(jnp.where(top, rh, pltpu.roll(ih, 4, 0)), 64, 1),
                    pltpu.roll(jnp.where(top, pltpu.roll(rh, 4, 0), ih), 96, 1),
                ]
                both.append(groups)
            for zt in range(4):
                halves = []
                for groups in both:
                    r = groups[3]
                    for g in range(3):
                        r = jnp.where(lane_block == (zt + g) % 4, groups[g], r)
                    halves.append(r)
                wsend[t, zt, cp] = jnp.concatenate(halves, axis=0).astype(BF16)

    for cp in range(4):
        whiten(cp)
        if cp == 0:
            pl.semaphore_wait(barrier, 42)
    for oy in (4, 3, 5, 2, 6, 1, 7, 0):
        for oz in (2, 1, 3, 0):
            if oy or oz:
                spread(oy, oz, y, z).start()
    line[z, y] = wsend[y, z]

    lanes = lax.broadcasted_iota(jnp.int32, (1, 128), 1)

    def select(d):
        def fill(j, carry):
            hit = jnp.where(lanes == pair_ref[d, j % 8, j // 8], 1.0, 0.0)
            selt[d, pl.ds(j, 1), :] = hit
            selt[d, pl.ds(j + 64, 1), :] = hit
            return carry

        lax.fori_loop(0, 64, fill, 0)

    def find_slots():
        owner = owner_ref[...].astype(F32)
        across = jnp.broadcast_to(owner, (128, 128))
        down = across.T
        rows_i = lax.broadcasted_iota(jnp.int32, (128, 128), 0)
        cols_i = lax.broadcasted_iota(jnp.int32, (128, 128), 1)
        ahead = jnp.where((across == down) & (rows_i < cols_i), 1.0, 0.0)
        slot = owner * 8.0 + jnp.sum(ahead, axis=0, keepdims=True)
        r = lax.broadcasted_iota(jnp.int32, (256, 128), 0)
        wanted = (((r >> 3) & 7) * 4 + ((r >> 6) & 1) * 2 + (r >> 7)) * 8 + (r & 7)
        pick[...] = jnp.where(wanted.astype(F32) == slot, 1.0, 0.0).astype(BF16)

    def combine(d):
        comb[d] = jnp.dot(
            pick[...], selt[d].T.astype(BF16), preferred_element_type=F32
        ).astype(BF16)

    def store_slots(v):
        for p in range(2):
            vbuf[:, :, :, p] = v[:, 128 * p:128 * p + 128].reshape(2, 2, 8, 8, 128)

    def arrive(b, oy):
        yo = (y + 8 - oy) % 8
        oz = (z + 4 - b) % 4

        def wait():
            spread(oy, oz, yo, b).wait_recv()

        if oy:
            wait()
        else:
            pl.when(z != b)(wait)
        if b < REACH:
            onward(b, oy).start()
        near[b, yo] = line[b, yo].astype(F32).reshape(8, 8, 128)

    sign = jnp.where(top, -1.0, 1.0)
    row8 = lax.broadcasted_iota(jnp.int32, (8, 128), 0)

    def halve(a, b, mask, by, axis):
        return jnp.where(mask, a, b) + pltpu.roll(jnp.where(mask, b, a), by, axis)

    def sum_rows(q):
        for by in (1, 2, 4):
            mask = (row8 & by) == 0
            q = [halve(q[2 * i], q[2 * i + 1], mask, by, 0) for i in range(len(q) // 2)]
        return q[0]

    def sum_groups(q):
        for by in (1, 2):
            mask = (lane_block & by) == 0
            q = [halve(q[2 * i], q[2 * i + 1], mask, 32 * by, 1) for i in range(len(q) // 2)]
        return q[0]

    def products(i, far, b):
        def body(kp, carry):
            re = [[None] * 8, [None] * 8]
            im = [[None] * 8, [None] * 8]
            for w in range(8):
                pair = far[b, w, kp].astype(F32)
                f = [pair[:8], pair[8:]]
                g = [pltpu.roll(q, 4, 0) * sign for q in f]
                for c in range(8):
                    a = near[i, w, c]
                    for h in range(2):
                        pr = a * f[h]
                        pi = a * g[h]
                        re[h][c] = pr if w == 0 else re[h][c] + pr
                        im[h][c] = pi if w == 0 else im[h][c] + pi
            for h in range(2):
                sums[0, h, kp] = sum_rows(re[h])
                sums[1, h, kp] = sum_rows(im[h])
            return carry

        lax.fori_loop(0, 4, body, 0)

    block16 = lax.broadcasted_iota(jnp.int32, (16, 128), 1) >> 5

    def split(rows):
        hi = rows.astype(BF16)
        return hi, (rows - hi.astype(F32)).astype(BF16)

    def fold(i, d):
        for p in range(2):
            for h in range(2):
                msg[i, d, p, 8 * h:8 * h + 8] = sum_groups([sums[p, h, g] for g in range(4)])

    def home(i, origin):
        return remote(msg.at[i], rin.at[origin], ms.at[i], mr.at[origin], (x * 4 + i, win))

    def send_home(i):
        @pl.when(z != i)
        def _():
            home(i, z).start()

    def cross(i, d):
        if i + d < 4:
            products(i, line, i + d)
        else:
            products(i, ahead_line, i + d - 4)
        fold(i, d)

    select(0)
    select(1)
    for oy in (0, 1, 7, 2, 6, 3, 5, 4):
        for b in range(2):
            arrive(b, oy)
    for oy in (0, 1, 7, 2, 6, 3, 5, 4):
        for b in range(2, 4):
            arrive(b, oy)
    for d in range(3):
        cross(0, d)
    send_home(0)
    for d in range(3):
        cross(1, d)
    send_home(1)
    cross(2, 0)
    cross(2, 1)
    cross(3, 0)
    select(2)
    find_slots()
    for d in range(3):
        combine(d)
    for oy in range(8):
        onward(0, oy).wait_recv()
    cross(3, 1)
    for oy in range(8):
        onward(1, oy).wait_recv()
    cross(3, 2)
    send_home(3)
    cross(2, 2)
    send_home(2)
    rin[z] = msg[z]
    for i in range(4):
        @pl.when(z != i)
        def _(i=i):
            home(i, i).wait_recv()

    v = None
    for d in range(3):
        parts = []
        for p in range(2):
            got = []
            for g in range(4):
                r = pltpu.roll(rin[3, d, p], 32 * ((3 - g) % 4), 1) if g != 3 else rin[3, d, p]
                for o in range(3):
                    q = rin[o, d, p]
                    if o != g:
                        q = pltpu.roll(q, 32 * ((o - g) % 4), 1)
                    r = jnp.where(block16 == o, q, r)
                got.append(r)
            parts.append(jnp.concatenate(got, axis=0))
        hi, lo = split(jnp.concatenate(parts, axis=1))
        term = jnp.dot(comb[d], jnp.concatenate([hi, lo], axis=0), preferred_element_type=F32)
        v = term if d == 0 else v + term
    store_slots(v * factor)

    def core_copy(i):
        z = 1 - zh if i == 0 else zh
        return remote(vbuf.at[1 - core, z], cbuf.at[z], cs.at[i], cr.at[i], (chan, sibling))

    def slot_copy(i, dy, at, origin):
        z = 1 - zh if i == 0 else zh
        to = (y + dy) % 8
        m = 8 * i + dy
        return remote(
            vbuf.at[core, z, to], rbuf.at[at, origin], fs.at[m], fr.at[m],
            (chan, to * 4 + z * 2 + core),
        )

    for i in range(2):
        core_copy(i).start()
    for i in range(2):
        side = 1 - zh if i == 0 else zh
        core_copy(i).wait_recv()
        vbuf[core, side] += cbuf[side]
        for dy in (4, 3, 5, 2, 6, 1, 7, 0):
            if dy or i == 0:
                slot_copy(i, dy, zh, y).start()
    rbuf[zh, y] = vbuf[core, zh, y]
    for i in (1, 0):
        for dy in (1, 7, 2, 6, 3, 5, 4, 0):
            if dy or i == 0:
                slot_copy(i, dy, 1 - zh if i == 0 else zh, (y + 8 - dy) % 8).wait_recv()
    for t in range(8):
        for p in range(2):
            out_ref[p * 8 + t] = rbuf[0, t, p] + rbuf[1, t, p]

    for oy in range(8):
        for oz in range(4):
            if oy or oz:
                spread(oy, oz, y, z).wait_send()
        for b in range(REACH):
            onward(b, oy).wait_send()
    for i in range(4):
        @pl.when(z != i)
        def _(i=i):
            home(i, z).wait_send()
    for i in range(2):
        core_copy(i).wait_send()
        for dy in range(8):
            if dy or i == 0:
                slot_copy(i, dy, zh, y).wait_send()


def shards(n_chan, spectra, pair_bin, bin_owner):
    channels, windows, _, freqs = spectra.shape
    factor = math.sqrt(BINS_OWN / (windows * (REACH + 1) * channels * channels))
    rows = spectra.reshape(channels, windows, 2, freqs // 128, 128)
    rows = rows.transpose(0, 1, 3, 2, 4).reshape(channels, windows, 16, 128)
    vmem = pl.BlockSpec(memory_space=pltpu.VMEM)
    dma = pltpu.SemaphoreType.DMA
    out = pl.pallas_call(
        functools.partial(kernel, n_chan, factor),
        out_shape=jax.ShapeDtypeStruct((16, 8, 128), F32),
        in_specs=[pl.BlockSpec(memory_space=pl.ANY), pl.BlockSpec(memory_space=pltpu.SMEM), vmem],
        out_specs=vmem,
        scratch_shapes=[
            pltpu.VMEM((8, 16, 16, 128), BF16),
            pltpu.VMEM((2, 256, 128), F32),
            pltpu.VMEM((8, 4, 4, 16, 128), BF16),
            pltpu.VMEM((4, 8, 4, 16, 128), BF16),
            pltpu.VMEM((2, 8, 4, 16, 128), BF16),
            pltpu.VMEM((4, 8, 8, 8, 128), F32),
            pltpu.VMEM((2, 2, 4, 8, 128), F32),
            pltpu.VMEM((4, 3, 2, 16, 128), F32),
            pltpu.VMEM((4, 3, 2, 16, 128), F32),
            pltpu.VMEM((3, 128, 128), F32),
            pltpu.VMEM((256, 128), BF16),
            pltpu.VMEM((3, 256, 128), BF16),
            pltpu.VMEM((2, 2, 8, 2, 8, 128), F32),
            pltpu.VMEM((2, 8, 2, 8, 128), F32),
            pltpu.VMEM((2, 8, 2, 8, 128), F32),
            dma((8,)), dma((32,)), dma((32,)), dma((16,)), dma((16,)), dma((4,)), dma((4,)),
            dma((2,)), dma((2,)), dma((16,)), dma((16,)),
        ],
        compiler_params=pltpu.CompilerParams(
            collective_id=0, has_side_effects=True, vmem_limit_bytes=60 * 1024 * 1024
        ),
    )(rows, pair_bin.transpose(1, 0, 2), bin_owner.reshape(1, 128))
    out = out[:, :CAP].reshape(2, 8, CAP, 128).transpose(2, 0, 1, 3)
    return out.reshape(1, CAP, 2, freqs)


def solution(mesh):
    in_specs = (P("chan", "win", None, None), P("chan", None, None), P())
    out_specs = P("chan", "win", None, None)
    body = functools.partial(shards, mesh.shape["chan"])
    return jax.shard_map(body, mesh=mesh, in_specs=in_specs, out_specs=out_specs, check_vma=False)
```

```python
import functools
import math

import jax
import jax.numpy as jnp
from jax import lax
from jax.experimental import pallas as pl
from jax.experimental.pallas import tpu as pltpu
from jax.sharding import PartitionSpec as P

REACH = 2
BINS_OWN = 4
CAP = 7
EPS = 1e-06
F32 = jnp.float32
BF16 = jnp.bfloat16


def kernel(
    n_chan, factor,
    spec_hbm, pair_ref, owner_ref, out_ref,
    spec, tmp, wsend, line, ahead_line, near, sums, msg, rin, selt, pick, comb, vbuf, cbuf, rbuf,
    ins, ats, atr, xs, xr, ms, mr, cs, cr, fs, fr,
):
    chan = lax.axis_index("chan")
    win = lax.axis_index("win")
    x = chan // 4
    z = chan % 4
    core = win % 2
    chip = win // 2
    y = chip // 2
    zh = chip % 2
    inner = win % 4
    n_x = n_chan // 4
    x_left = (x + n_x - 1) % n_x
    x_right = (x + 1) % n_x
    sibling = win + 1 - 2 * core
    mesh_id = pl.DeviceIdType.MESH

    barrier = pltpu.get_barrier_semaphore()

    def greet(c, w):
        pl.semaphore_signal(barrier, inc=1, device_id=(c, w), device_id_type=mesh_id)

    for c in range(8):
        pltpu.make_async_copy(spec_hbm.at[c], spec.at[c], ins.at[c]).start()
    for near_x in (x_left, x_right):
        greet(near_x * 4 + z, win)
    greet(chan, sibling)
    for oy in range(8):
        for oz in range(4):
            if oy or oz:
                greet(x * 4 + (z + oz) % 4, ((y + oy) % 8) * 4 + inner)
        greet(chan, ((y + oy) % 8) * 4 + (1 - zh) * 2 + core)

    def remote(src, dst, send, recv, to):
        return pltpu.make_async_remote_copy(
            src_ref=src, dst_ref=dst, send_sem=send, recv_sem=recv, device_id=to, device_id_type=mesh_id
        )

    def spread(oy, oz, yo, zo):
        yt = (y + oy) % 8
        zt = (z + oz) % 4
        m = oy * 4 + oz
        return remote(
            wsend.at[yt, zt], line.at[zo, yo], ats.at[m], atr.at[m], (x * 4 + zt, yt * 4 + inner)
        )

    def onward(b, oy):
        yo = (y + 8 - oy) % 8
        m = b * 8 + oy
        return remote(line.at[b, yo], ahead_line.at[b, yo], xs.at[m], xr.at[m], (x_left * 4 + z, win))

    lane_block = lax.broadcasted_iota(jnp.int32, (8, 128), 1) >> 5
    top = lax.broadcasted_iota(jnp.int32, (8, 128), 0) < 4

    def whiten(cp):
        for i in range(2):
            c = 2 * cp + i
            pltpu.make_async_copy(spec_hbm.at[c], spec.at[c], ins.at[c]).wait()
            v = spec[c].astype(F32)
            power = jnp.sum(jnp.sum(v * v, axis=1, keepdims=True), axis=2, keepdims=True) * (1.0 / 2048.0)
            tmp[i] = (v * lax.rsqrt(power + EPS)).reshape(256, 128)
        for t in range(8):
            both = []
            for i in range(2):
                rl = tmp[i, pl.ds(2 * t, 8, stride=16), :]
                il = tmp[i, pl.ds(2 * t + 1, 8, stride=16), :]
                rh = tmp[i, pl.ds(128 + 2 * t, 8, stride=16), :]
                ih = tmp[i, pl.ds(129 + 2 * t, 8, stride=16), :]
                groups = [
                    jnp.where(top, rl, pltpu.roll(il, 4, 0)),
                    pltpu.roll(jnp.where(top, pltpu.roll(rl, 4, 0), il), 32, 1),
                    pltpu.roll(jnp.where(top, rh, pltpu.roll(ih, 4, 0)), 64, 1),
                    pltpu.roll(jnp.where(top, pltpu.roll(rh, 4, 0), ih), 96, 1),
                ]
                both.append(groups)
            for zt in range(4):
                halves = []
                for groups in both:
                    r = groups[3]
                    for g in range(3):
                        r = jnp.where(lane_block == (zt + g) % 4, groups[g], r)
                    halves.append(r)
                wsend[t, zt, cp] = jnp.concatenate(halves, axis=0).astype(BF16)

    for cp in range(4):
        whiten(cp)
        if cp == 0:
            pl.semaphore_wait(barrier, 42)
    for oz in (2, 1, 3, 0):
        for oy in (4, 3, 5, 2, 6, 1, 7, 0):
            if oy or oz:
                spread(oy, oz, y, z).start()
    line[z, y] = wsend[y, z]

    lanes = lax.broadcasted_iota(jnp.int32, (1, 128), 1)

    def select(d):
        def fill(j, carry):
            hit = jnp.where(lanes == pair_ref[d, j % 8, j // 8], 1.0, 0.0)
            selt[d, pl.ds(j, 1), :] = hit
            selt[d, pl.ds(j + 64, 1), :] = hit
            return carry

        lax.fori_loop(0, 64, fill, 0)

    def find_slots():
        owner = owner_ref[...].astype(F32)
        across = jnp.broadcast_to(owner, (128, 128))
        down = across.T
        rows_i = lax.broadcasted_iota(jnp.int32, (128, 128), 0)
        cols_i = lax.broadcasted_iota(jnp.int32, (128, 128), 1)
        ahead = jnp.where((across == down) & (rows_i < cols_i), 1.0, 0.0)
        slot = owner * 8.0 + jnp.sum(ahead, axis=0, keepdims=True)
        r = lax.broadcasted_iota(jnp.int32, (256, 128), 0)
        wanted = (((r >> 3) & 7) * 4 + ((r >> 6) & 1) * 2 + (r >> 7)) * 8 + (r & 7)
        pick[...] = jnp.where(wanted.astype(F32) == slot, 1.0, 0.0).astype(BF16)

    def combine(d):
        comb[d] = jnp.dot(
            pick[...], selt[d].T.astype(BF16), preferred_element_type=F32
        ).astype(BF16)

    def store_slots(v):
        for p in range(2):
            vbuf[:, :, :, p] = v[:, 128 * p:128 * p + 128].reshape(2, 2, 8, 8, 128)

    def arrive(b, oy):
        yo = (y + 8 - oy) % 8
        oz = (z + 4 - b) % 4

        def wait():
            spread(oy, oz, yo, b).wait_recv()

        if oy:
            wait()
        else:
            pl.when(z != b)(wait)
        if b < REACH:
            onward(b, oy).start()
        near[b, yo] = line[b, yo].astype(F32).reshape(8, 8, 128)

    sign = jnp.where(top, -1.0, 1.0)
    row8 = lax.broadcasted_iota(jnp.int32, (8, 128), 0)

    def halve(a, b, mask, by, axis):
        return jnp.where(mask, a, b) + pltpu.roll(jnp.where(mask, b, a), by, axis)

    def sum_rows(q):
        for by in (1, 2, 4):
            mask = (row8 & by) == 0
            q = [halve(q[2 * i], q[2 * i + 1], mask, by, 0) for i in range(len(q) // 2)]
        return q[0]

    def sum_groups(q):
        for by in (1, 2):
            mask = (lane_block & by) == 0
            q = [halve(q[2 * i], q[2 * i + 1], mask, 32 * by, 1) for i in range(len(q) // 2)]
        return q[0]

    def products(i, far, b):
        def body(kp, carry):
            re = [[None] * 8, [None] * 8]
            im = [[None] * 8, [None] * 8]
            for w in range(8):
                pair = far[b, w, kp].astype(F32)
                f = [pair[:8], pair[8:]]
                g = [pltpu.roll(q, 4, 0) * sign for q in f]
                for c in range(8):
                    a = near[i, w, c]
                    for h in range(2):
                        pr = a * f[h]
                        pi = a * g[h]
                        re[h][c] = pr if w == 0 else re[h][c] + pr
                        im[h][c] = pi if w == 0 else im[h][c] + pi
            for h in range(2):
                sums[0, h, kp] = sum_rows(re[h])
                sums[1, h, kp] = sum_rows(im[h])
            return carry

        lax.fori_loop(0, 4, body, 0)

    block16 = lax.broadcasted_iota(jnp.int32, (16, 128), 1) >> 5

    def split(rows):
        hi = rows.astype(BF16)
        return hi, (rows - hi.astype(F32)).astype(BF16)

    def fold(i, d):
        for p in range(2):
            for h in range(2):
                msg[i, d, p, 8 * h:8 * h + 8] = sum_groups([sums[p, h, g] for g in range(4)])

    def home(i, origin):
        return remote(msg.at[i], rin.at[origin], ms.at[i], mr.at[origin], (x * 4 + i, win))

    def send_home(i):
        @pl.when(z != i)
        def _():
            home(i, z).start()

    def cross(i, d):
        if i + d < 4:
            products(i, line, i + d)
        else:
            products(i, ahead_line, i + d - 4)
        fold(i, d)

    select(0)
    select(1)
    select(2)
    find_slots()
    for d in range(3):
        combine(d)
    for oy in (4, 3, 5, 2, 6, 1, 7, 0):
        for b in range(2):
            arrive(b, oy)
    for oy in (4, 3, 5, 2, 6, 1, 7, 0):
        for b in range(2, 4):
            arrive(b, oy)
    for d in range(3):
        cross(0, d)
    send_home(0)
    for d in range(3):
        cross(1, d)
    send_home(1)
    cross(2, 0)
    cross(2, 1)
    cross(3, 0)
    for oy in range(8):
        onward(0, oy).wait_recv()
    cross(2, 2)
    send_home(2)
    cross(3, 1)
    for oy in range(8):
        onward(1, oy).wait_recv()
    cross(3, 2)
    send_home(3)
    rin[z] = msg[z]
    for i in range(4):
        @pl.when(z != i)
        def _(i=i):
            home(i, i).wait_recv()

    v = None
    for d in range(3):
        parts = []
        for p in range(2):
            got = []
            for g in range(4):
                r = pltpu.roll(rin[3, d, p], 32 * ((3 - g) % 4), 1) if g != 3 else rin[3, d, p]
                for o in range(3):
                    q = rin[o, d, p]
                    if o != g:
                        q = pltpu.roll(q, 32 * ((o - g) % 4), 1)
                    r = jnp.where(block16 == o, q, r)
                got.append(r)
            parts.append(jnp.concatenate(got, axis=0))
        hi, lo = split(jnp.concatenate(parts, axis=1))
        term = jnp.dot(comb[d], jnp.concatenate([hi, lo], axis=0), preferred_element_type=F32)
        v = term if d == 0 else v + term
    store_slots(v * factor)

    def core_copy(i):
        z = 1 - zh if i == 0 else zh
        return remote(vbuf.at[1 - core, z], cbuf.at[z], cs.at[i], cr.at[i], (chan, sibling))

    def slot_copy(i, dy, at, origin):
        z = 1 - zh if i == 0 else zh
        to = (y + dy) % 8
        m = 8 * i + dy
        return remote(
            vbuf.at[core, z, to], rbuf.at[at, origin], fs.at[m], fr.at[m],
            (chan, to * 4 + z * 2 + core),
        )

    for i in range(2):
        core_copy(i).start()
    for i in range(2):
        side = 1 - zh if i == 0 else zh
        core_copy(i).wait_recv()
        vbuf[core, side] += cbuf[side]
        for dy in (4, 3, 5, 2, 6, 1, 7, 0):
            if dy or i == 0:
                slot_copy(i, dy, zh, y).start()
    rbuf[zh, y] = vbuf[core, zh, y]
    for i in (1, 0):
        for dy in (1, 7, 2, 6, 3, 5, 4, 0):
            if dy or i == 0:
                slot_copy(i, dy, 1 - zh if i == 0 else zh, (y + 8 - dy) % 8).wait_recv()
    for t in range(8):
        for p in range(2):
            out_ref[p * 8 + t] = rbuf[0, t, p] + rbuf[1, t, p]

    for oy in range(8):
        for oz in range(4):
            if oy or oz:
                spread(oy, oz, y, z).wait_send()
        for b in range(REACH):
            onward(b, oy).wait_send()
    for i in range(4):
        @pl.when(z != i)
        def _(i=i):
            home(i, z).wait_send()
    for i in range(2):
        core_copy(i).wait_send()
        for dy in range(8):
            if dy or i == 0:
                slot_copy(i, dy, zh, y).wait_send()


def shards(n_chan, spectra, pair_bin, bin_owner):
    channels, windows, _, freqs = spectra.shape
    factor = math.sqrt(BINS_OWN / (windows * (REACH + 1) * channels * channels))
    rows = spectra.reshape(channels, windows, 2, freqs // 128, 128)
    rows = rows.transpose(0, 1, 3, 2, 4).reshape(channels, windows, 16, 128)
    vmem = pl.BlockSpec(memory_space=pltpu.VMEM)
    dma = pltpu.SemaphoreType.DMA
    out = pl.pallas_call(
        functools.partial(kernel, n_chan, factor),
        out_shape=jax.ShapeDtypeStruct((16, 8, 128), F32),
        in_specs=[pl.BlockSpec(memory_space=pl.ANY), pl.BlockSpec(memory_space=pltpu.SMEM), vmem],
        out_specs=vmem,
        scratch_shapes=[
            pltpu.VMEM((8, 16, 16, 128), BF16),
            pltpu.VMEM((2, 256, 128), F32),
            pltpu.VMEM((8, 4, 4, 16, 128), BF16),
            pltpu.VMEM((4, 8, 4, 16, 128), BF16),
            pltpu.VMEM((2, 8, 4, 16, 128), BF16),
            pltpu.VMEM((4, 8, 8, 8, 128), F32),
            pltpu.VMEM((2, 2, 4, 8, 128), F32),
            pltpu.VMEM((4, 3, 2, 16, 128), F32),
            pltpu.VMEM((4, 3, 2, 16, 128), F32),
            pltpu.VMEM((3, 128, 128), F32),
            pltpu.VMEM((256, 128), BF16),
            pltpu.VMEM((3, 256, 128), BF16),
            pltpu.VMEM((2, 2, 8, 2, 8, 128), F32),
            pltpu.VMEM((2, 8, 2, 8, 128), F32),
            pltpu.VMEM((2, 8, 2, 8, 128), F32),
            dma((8,)), dma((32,)), dma((32,)), dma((16,)), dma((16,)), dma((4,)), dma((4,)),
            dma((2,)), dma((2,)), dma((16,)), dma((16,)),
        ],
        compiler_params=pltpu.CompilerParams(
            collective_id=0, has_side_effects=True, vmem_limit_bytes=60 * 1024 * 1024
        ),
    )(rows, pair_bin.transpose(1, 0, 2), bin_owner.reshape(1, 128))
    out = out[:, :CAP].reshape(2, 8, CAP, 128).transpose(2, 0, 1, 3)
    return out.reshape(1, CAP, 2, freqs)


def solution(mesh):
    in_specs = (P("chan", "win", None, None), P("chan", None, None), P())
    out_specs = P("chan", "win", None, None)
    body = functools.partial(shards, mesh.shape["chan"])
    return jax.shard_map(body, mesh=mesh, in_specs=in_specs, out_specs=out_specs, check_vma=False)
```

```python
import functools
import math

import jax
import jax.numpy as jnp
from jax import lax
from jax.experimental import pallas as pl
from jax.experimental.pallas import tpu as pltpu
from jax.sharding import PartitionSpec as P

REACH = 2
BINS_OWN = 4
CAP = 7
EPS = 1e-06
F32 = jnp.float32
BF16 = jnp.bfloat16


def kernel(
    n_chan, factor,
    spec_hbm, pair_hbm, owner_hbm, out_ref,
    pair_ref, owner_ref, small, flat,
    spec, tmp, wsend, line, ahead_line, near, sums, msg, rin, selt, pick, comb, vbuf, cbuf, rbuf,
    ins, ats, atr, xs, xr, ms, mr, cs, cr, fs, fr,
):
    chan = lax.axis_index("chan")
    win = lax.axis_index("win")
    x = chan // 4
    z = chan % 4
    core = win % 2
    chip = win // 2
    y = chip // 2
    zh = chip % 2
    inner = win % 4
    n_x = n_chan // 4
    x_left = (x + n_x - 1) % n_x
    x_right = (x + 1) % n_x
    sibling = win + 1 - 2 * core
    mesh_id = pl.DeviceIdType.MESH

    barrier = pltpu.get_barrier_semaphore()

    def greet(c, w):
        pl.semaphore_signal(barrier, inc=1, device_id=(c, w), device_id_type=mesh_id)

    for c in range(8):
        pltpu.make_async_copy(spec_hbm.at[c], spec.at[c], ins.at[c]).start()
    pairs_in = pltpu.make_async_copy(pair_hbm, pair_ref, small.at[0])
    owners_in = pltpu.make_async_copy(owner_hbm, owner_ref, small.at[1])
    pairs_in.start()
    owners_in.start()
    for near_x in (x_left, x_right):
        greet(near_x * 4 + z, win)
    greet(chan, sibling)
    for oy in range(8):
        for oz in range(4):
            if oy or oz:
                greet(x * 4 + (z + oz) % 4, ((y + oy) % 8) * 4 + inner)
        greet(chan, ((y + oy) % 8) * 4 + (1 - zh) * 2 + core)

    def remote(src, dst, send, recv, to):
        return pltpu.make_async_remote_copy(
            src_ref=src, dst_ref=dst, send_sem=send, recv_sem=recv, device_id=to, device_id_type=mesh_id
        )

    def spread(oy, oz, yo, zo):
        yt = (y + oy) % 8
        zt = (z + oz) % 4
        m = oy * 4 + oz
        return remote(
            wsend.at[yt, zt], line.at[zo, yo], ats.at[m], atr.at[m], (x * 4 + zt, yt * 4 + inner)
        )

    def onward(b, oy):
        yo = (y + 8 - oy) % 8
        m = b * 8 + oy
        return remote(line.at[b, yo], ahead_line.at[b, yo], xs.at[m], xr.at[m], (x_left * 4 + z, win))

    lane_block = lax.broadcasted_iota(jnp.int32, (8, 128), 1) >> 5
    top = lax.broadcasted_iota(jnp.int32, (8, 128), 0) < 4

    def whiten(cp):
        for i in range(2):
            c = 2 * cp + i
            pltpu.make_async_copy(spec_hbm.at[c], spec.at[c], ins.at[c]).wait()
            v = spec[c].astype(F32)
            power = jnp.sum(jnp.sum(v * v, axis=1, keepdims=True), axis=2, keepdims=True) * (1.0 / 2048.0)
            tmp[i] = (v * lax.rsqrt(power + EPS)).reshape(256, 128)
        for t in range(8):
            both = []
            for i in range(2):
                rl = tmp[i, pl.ds(2 * t, 8, stride=16), :]
                il = tmp[i, pl.ds(2 * t + 1, 8, stride=16), :]
                rh = tmp[i, pl.ds(128 + 2 * t, 8, stride=16), :]
                ih = tmp[i, pl.ds(129 + 2 * t, 8, stride=16), :]
                groups = [
                    jnp.where(top, rl, pltpu.roll(il, 4, 0)),
                    pltpu.roll(jnp.where(top, pltpu.roll(rl, 4, 0), il), 32, 1),
                    pltpu.roll(jnp.where(top, rh, pltpu.roll(ih, 4, 0)), 64, 1),
                    pltpu.roll(jnp.where(top, pltpu.roll(rh, 4, 0), ih), 96, 1),
                ]
                both.append(groups)
            for zt in range(4):
                halves = []
                for groups in both:
                    r = groups[3]
                    for g in range(3):
                        r = jnp.where(lane_block == (zt + g) % 4, groups[g], r)
                    halves.append(r)
                wsend[t, zt, cp] = jnp.concatenate(halves, axis=0).astype(BF16)

    for cp in range(4):
        whiten(cp)
        if cp == 3:
            pl.semaphore_wait(barrier, 42)
    for oz in (2, 1, 3, 0):
        for oy in (4, 3, 5, 2, 6, 1, 7, 0):
            if oy or oz:
                spread(oy, oz, y, z).start()
    line[z, y] = wsend[y, z]

    lanes = lax.broadcasted_iota(jnp.int32, (1, 128), 1)

    def select(d):
        def fill(j, carry):
            hit = jnp.where(lanes == pair_ref[d, j % 8, j // 8], 1.0, 0.0)
            selt[d, pl.ds(j, 1), :] = hit
            selt[d, pl.ds(j + 64, 1), :] = hit
            return carry

        lax.fori_loop(0, 64, fill, 0)

    def select_own():
        def fill(j, carry):
            c, k = j % 8, j // 8
            hit = jnp.where(lanes == pair_ref[0, c, k], 1.0, 0.0)
            swap = jnp.where(lanes == pair_ref[0, k, c], 1.0, 0.0) * jnp.where(k > c, 1.0, 0.0)
            for part, r in enumerate((hit + swap, hit - swap)):
                selt[3 * part, pl.ds(j, 1), :] = r
                selt[3 * part, pl.ds(j + 64, 1), :] = r
            return carry

        lax.fori_loop(0, 64, fill, 0)

    def find_slots():
        owner = owner_ref[...].astype(F32)
        across = jnp.broadcast_to(owner, (128, 128))
        down = across.T
        rows_i = lax.broadcasted_iota(jnp.int32, (128, 128), 0)
        cols_i = lax.broadcasted_iota(jnp.int32, (128, 128), 1)
        ahead = jnp.where((across == down) & (rows_i < cols_i), 1.0, 0.0)
        slot = owner * 8.0 + jnp.sum(ahead, axis=0, keepdims=True)
        r = lax.broadcasted_iota(jnp.int32, (256, 128), 0)
        wanted = (((r >> 3) & 7) * 4 + ((r >> 6) & 1) * 2 + (r >> 7)) * 8 + (r & 7)
        pick[...] = jnp.where(wanted.astype(F32) == slot, 1.0, 0.0).astype(BF16)

    def combine(d):
        comb[d] = jnp.dot(
            pick[...], selt[d].T.astype(BF16), preferred_element_type=F32
        ).astype(BF16)

    def store_slots(v):
        for p in range(2):
            vbuf[:, :, :, p] = v[:, 128 * p:128 * p + 128].reshape(2, 2, 8, 8, 128)

    def arrive(b, oy):
        yo = (y + 8 - oy) % 8
        oz = (z + 4 - b) % 4

        def wait():
            spread(oy, oz, yo, b).wait_recv()

        if oy:
            wait()
        else:
            pl.when(z != b)(wait)
        if b < REACH:
            onward(b, oy).start()
        near[b, yo] = line[b, yo].astype(F32).reshape(8, 8, 128)

    sign = jnp.where(top, -1.0, 1.0)
    row8 = lax.broadcasted_iota(jnp.int32, (8, 128), 0)

    def halve(a, b, mask, by, axis):
        return jnp.where(mask, a, b) + pltpu.roll(jnp.where(mask, b, a), by, axis)

    def sum_rows(q):
        for by in (1, 2, 4):
            mask = (row8 & by) == 0
            q = [halve(q[2 * i], q[2 * i + 1], mask, by, 0) for i in range(len(q) // 2)]
        return q[0]

    def sum_groups(q):
        for by in (1, 2):
            mask = (lane_block & by) == 0
            q = [halve(q[2 * i], q[2 * i + 1], mask, 32 * by, 1) for i in range(len(q) // 2)]
        return q[0]

    def products(i, far, b):
        def body(kp, carry):
            count = [2 * kp + 1, 2 * kp + 2] if far is line and b == i else [8, 8]
            re = [[jnp.zeros((8, 128), F32)] * 8, [jnp.zeros((8, 128), F32)] * 8]
            im = [[jnp.zeros((8, 128), F32)] * 8, [jnp.zeros((8, 128), F32)] * 8]
            for w in range(8):
                pair = far[b, w, kp].astype(F32)
                f = [pair[:8], pair[8:]]
                g = [pltpu.roll(q, 4, 0) * sign for q in f]
                for c in range(count[1]):
                    a = near[i, w, c]
                    for h in range(2):
                        if c < count[h]:
                            pr = a * f[h]
                            pi = a * g[h]
                            re[h][c] = pr if w == 0 else re[h][c] + pr
                            im[h][c] = pi if w == 0 else im[h][c] + pi
            for h in range(2):
                sums[0, h, kp] = sum_rows(re[h])
                sums[1, h, kp] = sum_rows(im[h])
            return carry

        if far is line and b == i:
            for kp in range(4):
                body(kp, 0)
        else:
            lax.fori_loop(0, 4, body, 0)

    block16 = lax.broadcasted_iota(jnp.int32, (16, 128), 1) >> 5

    def split(rows):
        hi = rows.astype(BF16)
        return hi, (rows - hi.astype(F32)).astype(BF16)

    def fold(i, d):
        for p in range(2):
            for h in range(2):
                msg[i, d, p, 8 * h:8 * h + 8] = sum_groups([sums[p, h, g] for g in range(4)])

    def home(i, origin):
        return remote(msg.at[i], rin.at[origin], ms.at[i], mr.at[origin], (x * 4 + i, win))

    def send_home(i):
        @pl.when(z != i)
        def _():
            home(i, z).start()

    def cross(i, d):
        if i + d < 4:
            products(i, line, i + d)
        else:
            products(i, ahead_line, i + d - 4)
        fold(i, d)

    pairs_in.wait()
    owners_in.wait()
    select_own()
    select(1)
    select(2)
    find_slots()
    for d in range(4):
        combine(d)
    for oy in (4, 3, 5, 2, 6, 1, 7, 0):
        for b in range(2):
            arrive(b, oy)
    for oy in (4, 3, 5, 2, 6, 1, 7, 0):
        for b in range(2, 4):
            arrive(b, oy)
    for d in range(3):
        cross(0, d)
    send_home(0)
    for d in range(3):
        cross(1, d)
    send_home(1)
    cross(2, 0)
    cross(2, 1)
    cross(3, 0)
    for oy in range(8):
        onward(0, oy).wait_recv()
    cross(2, 2)
    send_home(2)
    cross(3, 1)
    for oy in range(8):
        onward(1, oy).wait_recv()
    cross(3, 2)
    send_home(3)
    rin[z] = msg[z]
    for i in range(4):
        @pl.when(z != i)
        def _(i=i):
            home(i, i).wait_recv()

    v = None
    for d in range(3):
        parts = []
        for p in range(2):
            got = []
            for g in range(4):
                r = pltpu.roll(rin[3, d, p], 32 * ((3 - g) % 4), 1) if g != 3 else rin[3, d, p]
                for o in range(3):
                    q = rin[o, d, p]
                    if o != g:
                        q = pltpu.roll(q, 32 * ((o - g) % 4), 1)
                    r = jnp.where(block16 == o, q, r)
                got.append(r)
            parts.append(jnp.concatenate(got, axis=0))
        hi, lo = split(jnp.concatenate(parts, axis=1))
        both = jnp.concatenate([hi, lo], axis=0)
        if d == 0:
            term = jnp.concatenate(
                [
                    jnp.dot(comb[3 * p], both[:, 128 * p:128 * p + 128], preferred_element_type=F32)
                    for p in range(2)
                ],
                axis=1,
            )
        else:
            term = jnp.dot(comb[d], both, preferred_element_type=F32)
        v = term if d == 0 else v + term
    store_slots(v * factor)

    def core_copy(i):
        z = 1 - zh if i == 0 else zh
        return remote(vbuf.at[1 - core, z], cbuf.at[z], cs.at[i], cr.at[i], (chan, sibling))

    def slot_copy(i, dy, at, origin):
        z = 1 - zh if i == 0 else zh
        to = (y + dy) % 8
        m = 8 * i + dy
        return remote(
            vbuf.at[core, z, to], rbuf.at[at, origin], fs.at[m], fr.at[m],
            (chan, to * 4 + z * 2 + core),
        )

    for i in range(2):
        core_copy(i).start()
    for i in range(2):
        side = 1 - zh if i == 0 else zh
        core_copy(i).wait_recv()
        vbuf[core, side] += cbuf[side]
        for dy in (4, 3, 5, 2, 6, 1, 7, 0):
            if dy or i == 0:
                slot_copy(i, dy, zh, y).start()
    rbuf[zh, y] = vbuf[core, zh, y]
    for i in (1, 0):
        for dy in (1, 7, 2, 6, 3, 5, 4, 0):
            if dy or i == 0:
                slot_copy(i, dy, 1 - zh if i == 0 else zh, (y + 8 - dy) % 8).wait_recv()
    for t in range(8):
        for p in range(2):
            flat[pl.ds(2 * t + p, 8, stride=16), :] = rbuf[0, t, p] + rbuf[1, t, p]
    out_ref[...] = flat[0:16 * CAP, :]

    for oy in range(8):
        for oz in range(4):
            if oy or oz:
                spread(oy, oz, y, z).wait_send()
        for b in range(REACH):
            onward(b, oy).wait_send()
    for i in range(4):
        @pl.when(z != i)
        def _(i=i):
            home(i, z).wait_send()
    for i in range(2):
        core_copy(i).wait_send()
        for dy in range(8):
            if dy or i == 0:
                slot_copy(i, dy, zh, y).wait_send()


def shards(n_chan, spectra, pair_bin, bin_owner):
    channels, windows, _, freqs = spectra.shape
    factor = math.sqrt(BINS_OWN / (windows * (REACH + 1) * channels * channels))
    rows = spectra.reshape(channels, windows, 2, freqs // 128, 128)
    rows = rows.transpose(0, 1, 3, 2, 4).reshape(channels, windows, 16, 128)
    vmem = pl.BlockSpec(memory_space=pltpu.VMEM)
    dma = pltpu.SemaphoreType.DMA
    out = pl.pallas_call(
        functools.partial(kernel, n_chan, factor),
        out_shape=jax.ShapeDtypeStruct((16 * CAP, 128), F32),
        in_specs=[pl.BlockSpec(memory_space=pl.ANY)] * 3,
        out_specs=vmem,
        scratch_shapes=[
            pltpu.SMEM((3, 8, 8), jnp.int32),
            pltpu.VMEM((1, 128), jnp.int32),
            dma((2,)),
            pltpu.VMEM((128, 128), F32),
            pltpu.VMEM((8, 16, 16, 128), BF16),
            pltpu.VMEM((2, 256, 128), F32),
            pltpu.VMEM((8, 4, 4, 16, 128), BF16),
            pltpu.VMEM((4, 8, 4, 16, 128), BF16),
            pltpu.VMEM((2, 8, 4, 16, 128), BF16),
            pltpu.VMEM((4, 8, 8, 8, 128), F32),
            pltpu.VMEM((2, 2, 4, 8, 128), F32),
            pltpu.VMEM((4, 3, 2, 16, 128), F32),
            pltpu.VMEM((4, 3, 2, 16, 128), F32),
            pltpu.VMEM((4, 128, 128), F32),
            pltpu.VMEM((256, 128), BF16),
            pltpu.VMEM((4, 256, 128), BF16),
            pltpu.VMEM((2, 2, 8, 2, 8, 128), F32),
            pltpu.VMEM((2, 8, 2, 8, 128), F32),
            pltpu.VMEM((2, 8, 2, 8, 128), F32),
            dma((8,)), dma((32,)), dma((32,)), dma((16,)), dma((16,)), dma((4,)), dma((4,)),
            dma((2,)), dma((2,)), dma((16,)), dma((16,)),
        ],
        compiler_params=pltpu.CompilerParams(
            collective_id=0, has_side_effects=True, vmem_limit_bytes=60 * 1024 * 1024
        ),
    )(rows, pair_bin.transpose(1, 0, 2), bin_owner.reshape(1, 128))
    out = out.reshape(CAP, 8, 2, 128).transpose(0, 2, 1, 3)
    return out.reshape(1, CAP, 2, freqs)


def solution(mesh):
    in_specs = (P("chan", "win", None, None), P("chan", None, None), P())
    out_specs = P("chan", "win", None, None)
    body = functools.partial(shards, mesh.shape["chan"])
    return jax.shard_map(body, mesh=mesh, in_specs=in_specs, out_specs=out_specs, check_vma=False)
```

```python
import functools
import math

import jax
import jax.numpy as jnp
from jax import lax
from jax.experimental import pallas as pl
from jax.experimental.pallas import tpu as pltpu
from jax.sharding import PartitionSpec as P

REACH = 2
BINS_OWN = 4
CAP = 7
EPS = 1e-06
F32 = jnp.float32
BF16 = jnp.bfloat16


def kernel(
    n_chan, factor,
    spec_hbm, pair_hbm, owner_hbm, out_ref,
    pair_ref, owner_ref, small, flat,
    spec, tmp, wsend, line, ahead_line, near, sums, msg, rin, selt, pick, comb, vbuf, cbuf, rbuf,
    ins, ats, atr, xs, xr, ms, mr, cs, cr, fs, fr,
):
    chan = lax.axis_index("chan")
    win = lax.axis_index("win")
    x = chan // 4
    z = chan % 4
    core = win % 2
    chip = win // 2
    y = chip // 2
    zh = chip % 2
    inner = win % 4
    n_x = n_chan // 4
    x_left = (x + n_x - 1) % n_x
    x_right = (x + 1) % n_x
    sibling = win + 1 - 2 * core
    mesh_id = pl.DeviceIdType.MESH

    barrier = pltpu.get_barrier_semaphore()

    def greet(c, w):
        pl.semaphore_signal(barrier, inc=1, device_id=(c, w), device_id_type=mesh_id)

    for c in range(8):
        pltpu.make_async_copy(spec_hbm.at[c], spec.at[c], ins.at[c]).start()
    pairs_in = pltpu.make_async_copy(pair_hbm, pair_ref, small.at[0])
    owners_in = pltpu.make_async_copy(owner_hbm, owner_ref, small.at[1])
    pairs_in.start()
    owners_in.start()
    for near_x in (x_left, x_right):
        greet(near_x * 4 + z, win)
    greet(chan, sibling)
    for oy in range(8):
        for oz in range(4):
            if oy or oz:
                greet(x * 4 + (z + oz) % 4, ((y + oy) % 8) * 4 + inner)
        greet(chan, ((y + oy) % 8) * 4 + (1 - zh) * 2 + core)

    def remote(src, dst, send, recv, to):
        return pltpu.make_async_remote_copy(
            src_ref=src, dst_ref=dst, send_sem=send, recv_sem=recv, device_id=to, device_id_type=mesh_id
        )

    def spread(oy, oz, yo, zo):
        yt = (y + oy) % 8
        zt = (z + oz) % 4
        m = oy * 4 + oz
        return remote(
            wsend.at[yt, zt], line.at[zo, yo], ats.at[m], atr.at[m], (x * 4 + zt, yt * 4 + inner)
        )

    def onward(b, oy):
        yo = (y + 8 - oy) % 8
        m = b * 8 + oy
        return remote(line.at[b, yo], ahead_line.at[b, yo], xs.at[m], xr.at[m], (x_left * 4 + z, win))

    lane_block = lax.broadcasted_iota(jnp.int32, (8, 128), 1) >> 5
    top = lax.broadcasted_iota(jnp.int32, (8, 128), 0) < 4

    def whiten(cp):
        for i in range(2):
            c = 2 * cp + i
            pltpu.make_async_copy(spec_hbm.at[c], spec.at[c], ins.at[c]).wait()
            v = spec[c].astype(F32)
            power = jnp.sum(jnp.sum(v * v, axis=1, keepdims=True), axis=2, keepdims=True) * (1.0 / 2048.0)
            tmp[i] = (v * lax.rsqrt(power + EPS)).reshape(256, 128)
        for t in range(8):
            both = []
            for i in range(2):
                rl = tmp[i, pl.ds(2 * t, 8, stride=16), :]
                il = tmp[i, pl.ds(2 * t + 1, 8, stride=16), :]
                rh = tmp[i, pl.ds(128 + 2 * t, 8, stride=16), :]
                ih = tmp[i, pl.ds(129 + 2 * t, 8, stride=16), :]
                groups = [
                    jnp.where(top, rl, pltpu.roll(il, 4, 0)),
                    pltpu.roll(jnp.where(top, pltpu.roll(rl, 4, 0), il), 32, 1),
                    pltpu.roll(jnp.where(top, rh, pltpu.roll(ih, 4, 0)), 64, 1),
                    pltpu.roll(jnp.where(top, pltpu.roll(rh, 4, 0), ih), 96, 1),
                ]
                both.append(groups)
            for zt in range(4):
                halves = []
                for groups in both:
                    r = groups[3]
                    for g in range(3):
                        r = jnp.where(lane_block == (zt + g) % 4, groups[g], r)
                    halves.append(r)
                wsend[t, zt, cp] = jnp.concatenate(halves, axis=0).astype(BF16)

    for cp in range(4):
        whiten(cp)
        if cp == 3:
            pl.semaphore_wait(barrier, 42)
    for oz in (2, 1, 3, 0):
        for oy in (4, 3, 5, 2, 6, 1, 7, 0):
            if oy or oz:
                spread(oy, oz, y, z).start()
    line[z, y] = wsend[y, z]

    lanes = lax.broadcasted_iota(jnp.int32, (1, 128), 1)

    def select(d):
        def fill(j, carry):
            hit = jnp.where(lanes == pair_ref[d, j % 8, j // 8], 1.0, 0.0)
            selt[d, pl.ds(j, 1), :] = hit
            selt[d, pl.ds(j + 64, 1), :] = hit
            return carry

        lax.fori_loop(0, 64, fill, 0)

    def select_own():
        def fill(j, carry):
            c, k = j % 8, j // 8
            hit = jnp.where(lanes == pair_ref[0, c, k], 1.0, 0.0)
            swap = jnp.where(lanes == pair_ref[0, k, c], 1.0, 0.0) * jnp.where(k > c, 1.0, 0.0)
            for part, r in enumerate((hit + swap, hit - swap)):
                selt[3 * part, pl.ds(j, 1), :] = r
                selt[3 * part, pl.ds(j + 64, 1), :] = r
            return carry

        lax.fori_loop(0, 64, fill, 0)

    def find_slots():
        owner = owner_ref[...].astype(F32)
        across = jnp.broadcast_to(owner, (128, 128))
        down = across.T
        rows_i = lax.broadcasted_iota(jnp.int32, (128, 128), 0)
        cols_i = lax.broadcasted_iota(jnp.int32, (128, 128), 1)
        ahead = jnp.where((across == down) & (rows_i < cols_i), 1.0, 0.0)
        slot = owner * 8.0 + jnp.sum(ahead, axis=0, keepdims=True)
        r = lax.broadcasted_iota(jnp.int32, (256, 128), 0)
        wanted = (((r >> 3) & 7) * 4 + ((r >> 6) & 1) * 2 + (r >> 7)) * 8 + (r & 7)
        pick[...] = jnp.where(wanted.astype(F32) == slot, 1.0, 0.0).astype(BF16)

    def combine(d):
        comb[d] = jnp.dot(
            pick[...], selt[d].T.astype(BF16), preferred_element_type=F32
        ).astype(BF16)

    def store_slots(v):
        for p in range(2):
            vbuf[:, :, :, p] = v[:, 128 * p:128 * p + 128].reshape(2, 2, 8, 8, 128)

    def arrive(b, oy):
        yo = (y + 8 - oy) % 8
        oz = (z + 4 - b) % 4

        def wait():
            spread(oy, oz, yo, b).wait_recv()

        if oy:
            wait()
        else:
            pl.when(z != b)(wait)
        if b < REACH:
            onward(b, oy).start()
        near[b, yo] = line[b, yo].astype(F32).reshape(8, 8, 128)

    sign = jnp.where(top, -1.0, 1.0)
    row8 = lax.broadcasted_iota(jnp.int32, (8, 128), 0)

    def halve(a, b, mask, by, axis):
        return jnp.where(mask, a, b) + pltpu.roll(jnp.where(mask, b, a), by, axis)

    def sum_rows(q):
        for by in (1, 2, 4):
            mask = (row8 & by) == 0
            q = [halve(q[2 * i], q[2 * i + 1], mask, by, 0) for i in range(len(q) // 2)]
        return q[0]

    def sum_groups(q):
        for by in (1, 2):
            mask = (lane_block & by) == 0
            q = [halve(q[2 * i], q[2 * i + 1], mask, 32 * by, 1) for i in range(len(q) // 2)]
        return q[0]

    def products(i, far, b):
        def body(kp, carry):
            count = [2 * kp + 1, 2 * kp + 2] if far is line and b == i else [8, 8]
            re = [[jnp.zeros((8, 128), F32)] * 8, [jnp.zeros((8, 128), F32)] * 8]
            im = [[jnp.zeros((8, 128), F32)] * 8, [jnp.zeros((8, 128), F32)] * 8]
            for w in range(8):
                pair = far[b, w, kp].astype(F32)
                f = [pair[:8], pair[8:]]
                g = [pltpu.roll(q, 4, 0) * sign for q in f]
                for c in range(count[1]):
                    a = near[i, w, c]
                    for h in range(2):
                        if c < count[h]:
                            pr = a * f[h]
                            pi = a * g[h]
                            re[h][c] = pr if w == 0 else re[h][c] + pr
                            im[h][c] = pi if w == 0 else im[h][c] + pi
            for h in range(2):
                sums[0, h, kp] = sum_rows(re[h])
                sums[1, h, kp] = sum_rows(im[h])
            return carry

        if far is line and b == i:
            for kp in range(4):
                body(kp, 0)
        else:
            lax.fori_loop(0, 4, body, 0)

    block16 = lax.broadcasted_iota(jnp.int32, (16, 128), 1) >> 5

    def split(rows):
        hi = rows.astype(BF16)
        return hi, (rows - hi.astype(F32)).astype(BF16)

    def fold(i, d):
        for p in range(2):
            for h in range(2):
                msg[i, d, p, 8 * h:8 * h + 8] = sum_groups([sums[p, h, g] for g in range(4)])

    def home(i, origin):
        return remote(msg.at[i], rin.at[origin], ms.at[i], mr.at[origin], (x * 4 + i, win))

    def send_home(i):
        @pl.when(z != i)
        def _():
            home(i, z).start()

    def cross(i, d):
        if i + d < 4:
            products(i, line, i + d)
        else:
            products(i, ahead_line, i + d - 4)
        fold(i, d)

    pairs_in.wait()
    owners_in.wait()
    select_own()
    select(1)
    select(2)
    find_slots()
    for d in range(4):
        combine(d)
    for oy in (1, 7, 0, 2, 6, 3, 5, 4):
        for b in range(2):
            arrive(b, oy)
    for oy in (4, 3, 5, 2, 6, 1, 7, 0):
        for b in range(2, 4):
            arrive(b, oy)
    for d in range(3):
        cross(0, d)
    send_home(0)
    for d in range(3):
        cross(1, d)
    send_home(1)
    cross(2, 0)
    cross(2, 1)
    cross(3, 0)
    for oy in range(8):
        onward(0, oy).wait_recv()
    cross(2, 2)
    send_home(2)
    cross(3, 1)
    for oy in range(8):
        onward(1, oy).wait_recv()
    cross(3, 2)
    send_home(3)
    rin[z] = msg[z]
    for i in range(4):
        @pl.when(z != i)
        def _(i=i):
            home(i, i).wait_recv()

    v = None
    for d in range(3):
        parts = []
        for p in range(2):
            got = []
            for g in range(4):
                r = pltpu.roll(rin[3, d, p], 32 * ((3 - g) % 4), 1) if g != 3 else rin[3, d, p]
                for o in range(3):
                    q = rin[o, d, p]
                    if o != g:
                        q = pltpu.roll(q, 32 * ((o - g) % 4), 1)
                    r = jnp.where(block16 == o, q, r)
                got.append(r)
            parts.append(jnp.concatenate(got, axis=0))
        hi, lo = split(jnp.concatenate(parts, axis=1))
        both = jnp.concatenate([hi, lo], axis=0)
        if d == 0:
            term = jnp.concatenate(
                [
                    jnp.dot(comb[3 * p], both[:, 128 * p:128 * p + 128], preferred_element_type=F32)
                    for p in range(2)
                ],
                axis=1,
            )
        else:
            term = jnp.dot(comb[d], both, preferred_element_type=F32)
        v = term if d == 0 else v + term
    store_slots(v * factor)

    def core_copy(i):
        z = 1 - zh if i == 0 else zh
        return remote(vbuf.at[1 - core, z], cbuf.at[z], cs.at[i], cr.at[i], (chan, sibling))

    def slot_copy(i, dy, at, origin):
        z = 1 - zh if i == 0 else zh
        to = (y + dy) % 8
        m = 8 * i + dy
        return remote(
            vbuf.at[core, z, to], rbuf.at[at, origin], fs.at[m], fr.at[m],
            (chan, to * 4 + z * 2 + core),
        )

    for i in range(2):
        core_copy(i).start()
    for i in range(2):
        side = 1 - zh if i == 0 else zh
        core_copy(i).wait_recv()
        vbuf[core, side] += cbuf[side]
        for dy in (4, 3, 5, 2, 6, 1, 7, 0):
            if dy or i == 0:
                slot_copy(i, dy, zh, y).start()
    rbuf[zh, y] = vbuf[core, zh, y]
    for i in (1, 0):
        for dy in (1, 7, 2, 6, 3, 5, 4, 0):
            if dy or i == 0:
                slot_copy(i, dy, 1 - zh if i == 0 else zh, (y + 8 - dy) % 8).wait_recv()
    for t in range(8):
        for p in range(2):
            flat[pl.ds(2 * t + p, 8, stride=16), :] = rbuf[0, t, p] + rbuf[1, t, p]
    out_ref[...] = flat[0:16 * CAP, :]

    for oy in range(8):
        for oz in range(4):
            if oy or oz:
                spread(oy, oz, y, z).wait_send()
        for b in range(REACH):
            onward(b, oy).wait_send()
    for i in range(4):
        @pl.when(z != i)
        def _(i=i):
            home(i, z).wait_send()
    for i in range(2):
        core_copy(i).wait_send()
        for dy in range(8):
            if dy or i == 0:
                slot_copy(i, dy, zh, y).wait_send()


def shards(n_chan, spectra, pair_bin, bin_owner):
    channels, windows, _, freqs = spectra.shape
    factor = math.sqrt(BINS_OWN / (windows * (REACH + 1) * channels * channels))
    rows = spectra.reshape(channels, windows, 2, freqs // 128, 128)
    rows = rows.transpose(0, 1, 3, 2, 4).reshape(channels, windows, 16, 128)
    vmem = pl.BlockSpec(memory_space=pltpu.VMEM)
    dma = pltpu.SemaphoreType.DMA
    out = pl.pallas_call(
        functools.partial(kernel, n_chan, factor),
        out_shape=jax.ShapeDtypeStruct((16 * CAP, 128), F32),
        in_specs=[pl.BlockSpec(memory_space=pl.ANY)] * 3,
        out_specs=vmem,
        scratch_shapes=[
            pltpu.SMEM((3, 8, 8), jnp.int32),
            pltpu.VMEM((1, 128), jnp.int32),
            dma((2,)),
            pltpu.VMEM((128, 128), F32),
            pltpu.VMEM((8, 16, 16, 128), BF16),
            pltpu.VMEM((2, 256, 128), F32),
            pltpu.VMEM((8, 4, 4, 16, 128), BF16),
            pltpu.VMEM((4, 8, 4, 16, 128), BF16),
            pltpu.VMEM((2, 8, 4, 16, 128), BF16),
            pltpu.VMEM((4, 8, 8, 8, 128), F32),
            pltpu.VMEM((2, 2, 4, 8, 128), F32),
            pltpu.VMEM((4, 3, 2, 16, 128), F32),
            pltpu.VMEM((4, 3, 2, 16, 128), F32),
            pltpu.VMEM((4, 128, 128), F32),
            pltpu.VMEM((256, 128), BF16),
            pltpu.VMEM((4, 256, 128), BF16),
            pltpu.VMEM((2, 2, 8, 2, 8, 128), F32),
            pltpu.VMEM((2, 8, 2, 8, 128), F32),
            pltpu.VMEM((2, 8, 2, 8, 128), F32),
            dma((8,)), dma((32,)), dma((32,)), dma((16,)), dma((16,)), dma((4,)), dma((4,)),
            dma((2,)), dma((2,)), dma((16,)), dma((16,)),
        ],
        compiler_params=pltpu.CompilerParams(
            collective_id=0, has_side_effects=True, vmem_limit_bytes=60 * 1024 * 1024
        ),
    )(rows, pair_bin.transpose(1, 0, 2), bin_owner.reshape(1, 128))
    out = out.reshape(CAP, 8, 2, 128).transpose(0, 2, 1, 3)
    return out.reshape(1, CAP, 2, freqs)


def solution(mesh):
    in_specs = (P("chan", "win", None, None), P("chan", None, None), P())
    out_specs = P("chan", "win", None, None)
    body = functools.partial(shards, mesh.shape["chan"])
    return jax.shard_map(body, mesh=mesh, in_specs=in_specs, out_specs=out_specs, check_vma=False)
```

```python
import functools
import math

import jax
import jax.numpy as jnp
from jax import lax
from jax.experimental import pallas as pl
from jax.experimental.pallas import tpu as pltpu
from jax.sharding import PartitionSpec as P

REACH = 2
BINS_OWN = 4
CAP = 7
EPS = 1e-06
F32 = jnp.float32
BF16 = jnp.bfloat16


def kernel(
    n_chan, factor,
    spec_hbm, pair_hbm, owner_hbm, out_ref,
    pair_ref, owner_ref, small, flat,
    spec, tmp, wsend, line, ahead_line, near, sums, msg, rin, selt, pick, comb, vbuf, cbuf, rbuf,
    ins, ats, atr, xs, xr, ms, mr, cs, cr, fs, fr,
):
    chan = lax.axis_index("chan")
    win = lax.axis_index("win")
    x = chan // 4
    z = chan % 4
    core = win % 2
    chip = win // 2
    y = chip // 2
    zh = chip % 2
    inner = win % 4
    n_x = n_chan // 4
    x_left = (x + n_x - 1) % n_x
    x_right = (x + 1) % n_x
    sibling = win + 1 - 2 * core
    mesh_id = pl.DeviceIdType.MESH

    barrier = pltpu.get_barrier_semaphore()

    def greet(c, w):
        pl.semaphore_signal(barrier, inc=1, device_id=(c, w), device_id_type=mesh_id)

    for c in range(8):
        pltpu.make_async_copy(spec_hbm.at[c], spec.at[c], ins.at[c]).start()
    pairs_in = pltpu.make_async_copy(pair_hbm, pair_ref, small.at[0])
    owners_in = pltpu.make_async_copy(owner_hbm, owner_ref, small.at[1])
    pairs_in.start()
    owners_in.start()
    for near_x in (x_left, x_right):
        greet(near_x * 4 + z, win)
    greet(chan, sibling)
    for oy in range(8):
        for oz in range(4):
            if oy or oz:
                greet(x * 4 + (z + oz) % 4, ((y + oy) % 8) * 4 + inner)
        greet(chan, ((y + oy) % 8) * 4 + (1 - zh) * 2 + core)

    def remote(src, dst, send, recv, to):
        return pltpu.make_async_remote_copy(
            src_ref=src, dst_ref=dst, send_sem=send, recv_sem=recv, device_id=to, device_id_type=mesh_id
        )

    def spread(oy, oz, yo, zo):
        yt = (y + oy) % 8
        zt = (z + oz) % 4
        m = oy * 4 + oz
        return remote(
            wsend.at[yt, zt], line.at[zo, yo], ats.at[m], atr.at[m], (x * 4 + zt, yt * 4 + inner)
        )

    def onward(b, oy):
        yo = (y + 8 - oy) % 8
        m = b * 8 + oy
        return remote(line.at[b, yo], ahead_line.at[b, yo], xs.at[m], xr.at[m], (x_left * 4 + z, win))

    lane_block = lax.broadcasted_iota(jnp.int32, (8, 128), 1) >> 5
    top = lax.broadcasted_iota(jnp.int32, (8, 128), 0) < 4

    def whiten(cp):
        for i in range(2):
            c = 2 * cp + i
            pltpu.make_async_copy(spec_hbm.at[c], spec.at[c], ins.at[c]).wait()
            v = spec[c].astype(F32)
            power = jnp.sum(jnp.sum(v * v, axis=1, keepdims=True), axis=2, keepdims=True) * (1.0 / 2048.0)
            tmp[i] = (v * lax.rsqrt(power + EPS)).reshape(256, 128)
        for t in range(8):
            both = []
            for i in range(2):
                rl = tmp[i, pl.ds(2 * t, 8, stride=16), :]
                il = tmp[i, pl.ds(2 * t + 1, 8, stride=16), :]
                rh = tmp[i, pl.ds(128 + 2 * t, 8, stride=16), :]
                ih = tmp[i, pl.ds(129 + 2 * t, 8, stride=16), :]
                groups = [
                    jnp.where(top, rl, pltpu.roll(il, 4, 0)),
                    pltpu.roll(jnp.where(top, pltpu.roll(rl, 4, 0), il), 32, 1),
                    pltpu.roll(jnp.where(top, rh, pltpu.roll(ih, 4, 0)), 64, 1),
                    pltpu.roll(jnp.where(top, pltpu.roll(rh, 4, 0), ih), 96, 1),
                ]
                both.append(groups)
            for zt in range(4):
                halves = []
                for groups in both:
                    r = groups[3]
                    for g in range(3):
                        r = jnp.where(lane_block == (zt + g) % 4, groups[g], r)
                    halves.append(r)
                wsend[t, zt, cp] = jnp.concatenate(halves, axis=0).astype(BF16)

    for cp in range(4):
        whiten(cp)
        if cp == 3:
            pl.semaphore_wait(barrier, 42)
    for oz in (2, 1, 3, 0):
        for oy in (4, 3, 5, 2, 6, 1, 7, 0):
            if oy or oz:
                spread(oy, oz, y, z).start()
    line[z, y] = wsend[y, z]

    lanes = lax.broadcasted_iota(jnp.int32, (1, 128), 1)

    def select(d):
        def fill(j, carry):
            hit = jnp.where(lanes == pair_ref[d, j % 8, j // 8], 1.0, 0.0)
            selt[d, pl.ds(j, 1), :] = hit
            selt[d, pl.ds(j + 64, 1), :] = hit
            return carry

        lax.fori_loop(0, 64, fill, 0)

    def select_own():
        def fill(j, carry):
            c, k = j % 8, j // 8
            hit = jnp.where(lanes == pair_ref[0, c, k], 1.0, 0.0)
            swap = jnp.where(lanes == pair_ref[0, k, c], 1.0, 0.0) * jnp.where(k > c, 1.0, 0.0)
            for part, r in enumerate((hit + swap, hit - swap)):
                selt[3 * part, pl.ds(j, 1), :] = r
                selt[3 * part, pl.ds(j + 64, 1), :] = r
            return carry

        lax.fori_loop(0, 64, fill, 0)

    def find_slots():
        owner = owner_ref[...].astype(F32)
        across = jnp.broadcast_to(owner, (128, 128))
        down = across.T
        rows_i = lax.broadcasted_iota(jnp.int32, (128, 128), 0)
        cols_i = lax.broadcasted_iota(jnp.int32, (128, 128), 1)
        ahead = jnp.where((across == down) & (rows_i < cols_i), 1.0, 0.0)
        slot = owner * 8.0 + jnp.sum(ahead, axis=0, keepdims=True)
        r = lax.broadcasted_iota(jnp.int32, (256, 128), 0)
        wanted = (((r >> 3) & 7) * 4 + ((r >> 6) & 1) * 2 + (r >> 7)) * 8 + (r & 7)
        pick[...] = jnp.where(wanted.astype(F32) == slot, 1.0, 0.0).astype(BF16)

    def combine(d):
        comb[d] = jnp.dot(
            pick[...], selt[d].T.astype(BF16), preferred_element_type=F32
        ).astype(BF16)

    def store_slots(v):
        for p in range(2):
            vbuf[:, :, :, p] = v[:, 128 * p:128 * p + 128].reshape(2, 2, 8, 8, 128)

    def arrive(b, oy):
        yo = (y + 8 - oy) % 8
        oz = (z + 4 - b) % 4

        def wait():
            spread(oy, oz, yo, b).wait_recv()

        if oy:
            wait()
        else:
            pl.when(z != b)(wait)
        if b < REACH:
            onward(b, oy).start()
        near[b, yo] = line[b, yo].astype(F32).reshape(8, 8, 128)

    sign = jnp.where(top, -1.0, 1.0)
    row8 = lax.broadcasted_iota(jnp.int32, (8, 128), 0)

    def halve(a, b, mask, by, axis):
        return jnp.where(mask, a, b) + pltpu.roll(jnp.where(mask, b, a), by, axis)

    def sum_rows(q):
        for by in (1, 2, 4):
            mask = (row8 & by) == 0
            q = [halve(q[2 * i], q[2 * i + 1], mask, by, 0) for i in range(len(q) // 2)]
        return q[0]

    def sum_groups(q):
        for by in (1, 2):
            mask = (lane_block & by) == 0
            q = [halve(q[2 * i], q[2 * i + 1], mask, 32 * by, 1) for i in range(len(q) // 2)]
        return q[0]

    def products(i, far, b):
        def body(kp, carry):
            count = [2 * kp + 1, 2 * kp + 2] if far is line and b == i else [8, 8]
            re = [[jnp.zeros((8, 128), F32)] * 8, [jnp.zeros((8, 128), F32)] * 8]
            im = [[jnp.zeros((8, 128), F32)] * 8, [jnp.zeros((8, 128), F32)] * 8]
            for w in range(8):
                pair = far[b, w, kp].astype(F32)
                f = [pair[:8], pair[8:]]
                g = [pltpu.roll(q, 4, 0) * sign for q in f]
                for c in range(count[1]):
                    a = near[i, w, c]
                    for h in range(2):
                        if c < count[h]:
                            pr = a * f[h]
                            pi = a * g[h]
                            re[h][c] = pr if w == 0 else re[h][c] + pr
                            im[h][c] = pi if w == 0 else im[h][c] + pi
            for h in range(2):
                sums[0, h, kp] = sum_rows(re[h])
                sums[1, h, kp] = sum_rows(im[h])
            return carry

        if far is line and b == i:
            for kp in range(4):
                body(kp, 0)
        else:
            lax.fori_loop(0, 4, body, 0)

    block16 = lax.broadcasted_iota(jnp.int32, (16, 128), 1) >> 5

    def split(rows):
        hi = rows.astype(BF16)
        return hi, (rows - hi.astype(F32)).astype(BF16)

    def fold(i, d):
        for p in range(2):
            for h in range(2):
                msg[i, d, p, 8 * h:8 * h + 8] = sum_groups([sums[p, h, g] for g in range(4)])

    def home(i, origin):
        return remote(msg.at[i], rin.at[origin], ms.at[i], mr.at[origin], (x * 4 + i, win))

    def send_home(i):
        @pl.when(z != i)
        def _():
            home(i, z).start()

    def cross(i, d):
        if i + d < 4:
            products(i, line, i + d)
        else:
            products(i, ahead_line, i + d - 4)
        fold(i, d)

    pairs_in.wait()
    owners_in.wait()
    select_own()
    select(1)
    select(2)
    find_slots()
    for d in range(4):
        combine(d)
    for oy in (1, 7, 0, 2, 6, 3, 5, 4):
        for b in range(2):
            arrive(b, oy)
    for oy in (1, 7, 0, 2, 6, 3, 5, 4):
        for b in range(2, 4):
            arrive(b, oy)
    for d in range(3):
        cross(0, d)
    send_home(0)
    for d in range(3):
        cross(1, d)
    send_home(1)
    cross(2, 0)
    cross(2, 1)
    cross(3, 0)
    for oy in range(8):
        onward(0, oy).wait_recv()
    cross(2, 2)
    send_home(2)
    cross(3, 1)
    for oy in range(8):
        onward(1, oy).wait_recv()
    cross(3, 2)
    send_home(3)
    rin[z] = msg[z]
    for i in range(4):
        @pl.when(z != i)
        def _(i=i):
            home(i, i).wait_recv()

    v = None
    for d in range(3):
        parts = []
        for p in range(2):
            got = []
            for g in range(4):
                r = pltpu.roll(rin[3, d, p], 32 * ((3 - g) % 4), 1) if g != 3 else rin[3, d, p]
                for o in range(3):
                    q = rin[o, d, p]
                    if o != g:
                        q = pltpu.roll(q, 32 * ((o - g) % 4), 1)
                    r = jnp.where(block16 == o, q, r)
                got.append(r)
            parts.append(jnp.concatenate(got, axis=0))
        hi, lo = split(jnp.concatenate(parts, axis=1))
        both = jnp.concatenate([hi, lo], axis=0)
        if d == 0:
            term = jnp.concatenate(
                [
                    jnp.dot(comb[3 * p], both[:, 128 * p:128 * p + 128], preferred_element_type=F32)
                    for p in range(2)
                ],
                axis=1,
            )
        else:
            term = jnp.dot(comb[d], both, preferred_element_type=F32)
        v = term if d == 0 else v + term
    store_slots(v * factor)

    def core_copy(i):
        z = 1 - zh if i == 0 else zh
        return remote(vbuf.at[1 - core, z], cbuf.at[z], cs.at[i], cr.at[i], (chan, sibling))

    def slot_copy(i, dy, at, origin):
        z = 1 - zh if i == 0 else zh
        to = (y + dy) % 8
        m = 8 * i + dy
        return remote(
            vbuf.at[core, z, to], rbuf.at[at, origin], fs.at[m], fr.at[m],
            (chan, to * 4 + z * 2 + core),
        )

    for i in range(2):
        core_copy(i).start()
    for i in range(2):
        side = 1 - zh if i == 0 else zh
        core_copy(i).wait_recv()
        vbuf[core, side] += cbuf[side]
        for dy in (4, 3, 5, 2, 6, 1, 7, 0):
            if dy or i == 0:
                slot_copy(i, dy, zh, y).start()
    rbuf[zh, y] = vbuf[core, zh, y]
    for i in (1, 0):
        for dy in (1, 7, 2, 6, 3, 5, 4, 0):
            if dy or i == 0:
                slot_copy(i, dy, 1 - zh if i == 0 else zh, (y + 8 - dy) % 8).wait_recv()
    for t in range(8):
        for p in range(2):
            flat[pl.ds(2 * t + p, 8, stride=16), :] = rbuf[0, t, p] + rbuf[1, t, p]
    out_ref[...] = flat[0:16 * CAP, :]

    for oy in range(8):
        for oz in range(4):
            if oy or oz:
                spread(oy, oz, y, z).wait_send()
        for b in range(REACH):
            onward(b, oy).wait_send()
    for i in range(4):
        @pl.when(z != i)
        def _(i=i):
            home(i, z).wait_send()
    for i in range(2):
        core_copy(i).wait_send()
        for dy in range(8):
            if dy or i == 0:
                slot_copy(i, dy, zh, y).wait_send()


def shards(n_chan, spectra, pair_bin, bin_owner):
    channels, windows, _, freqs = spectra.shape
    factor = math.sqrt(BINS_OWN / (windows * (REACH + 1) * channels * channels))
    rows = spectra.reshape(channels, windows, 2, freqs // 128, 128)
    rows = rows.transpose(0, 1, 3, 2, 4).reshape(channels, windows, 16, 128)
    vmem = pl.BlockSpec(memory_space=pltpu.VMEM)
    dma = pltpu.SemaphoreType.DMA
    out = pl.pallas_call(
        functools.partial(kernel, n_chan, factor),
        out_shape=jax.ShapeDtypeStruct((16 * CAP, 128), F32),
        in_specs=[pl.BlockSpec(memory_space=pl.ANY)] * 3,
        out_specs=vmem,
        scratch_shapes=[
            pltpu.SMEM((3, 8, 8), jnp.int32),
            pltpu.VMEM((1, 128), jnp.int32),
            dma((2,)),
            pltpu.VMEM((128, 128), F32),
            pltpu.VMEM((8, 16, 16, 128), BF16),
            pltpu.VMEM((2, 256, 128), F32),
            pltpu.VMEM((8, 4, 4, 16, 128), BF16),
            pltpu.VMEM((4, 8, 4, 16, 128), BF16),
            pltpu.VMEM((2, 8, 4, 16, 128), BF16),
            pltpu.VMEM((4, 8, 8, 8, 128), F32),
            pltpu.VMEM((2, 2, 4, 8, 128), F32),
            pltpu.VMEM((4, 3, 2, 16, 128), F32),
            pltpu.VMEM((4, 3, 2, 16, 128), F32),
            pltpu.VMEM((4, 128, 128), F32),
            pltpu.VMEM((256, 128), BF16),
            pltpu.VMEM((4, 256, 128), BF16),
            pltpu.VMEM((2, 2, 8, 2, 8, 128), F32),
            pltpu.VMEM((2, 8, 2, 8, 128), F32),
            pltpu.VMEM((2, 8, 2, 8, 128), F32),
            dma((8,)), dma((32,)), dma((32,)), dma((16,)), dma((16,)), dma((4,)), dma((4,)),
            dma((2,)), dma((2,)), dma((16,)), dma((16,)),
        ],
        compiler_params=pltpu.CompilerParams(
            collective_id=0, has_side_effects=True, vmem_limit_bytes=60 * 1024 * 1024
        ),
    )(rows, pair_bin.transpose(1, 0, 2), bin_owner.reshape(1, 128))
    out = out.reshape(CAP, 8, 2, 128).transpose(0, 2, 1, 3)
    return out.reshape(1, CAP, 2, freqs)


def solution(mesh):
    in_specs = (P("chan", "win", None, None), P("chan", None, None), P())
    out_specs = P("chan", "win", None, None)
    body = functools.partial(shards, mesh.shape["chan"])
    return jax.shard_map(body, mesh=mesh, in_specs=in_specs, out_specs=out_specs, check_vma=False)
```
